512 devices in a mesh: dp: 64 (over z, y_hi, core), tensor: 8 (over y_lo, x).
Axes of the slice: x: 4, y: 4 (y_hi: 2, y_lo: 2; y = y_hi * 2 + y_lo), z: 16, core: 2. Of those that a mesh axis runs over, the one named last changes fastest.
Arguments:
- tokens: bfloat16 [8192, 8192], P('dp', 'tensor'), may hold values from -6 to 6
- frozen_gate_up: bfloat16 [8192, 2, 15360], P('dp', None, 'tensor'), may hold values from -6 to 6
- frozen_down_factor: bfloat16 [4, 64, 8192], P(None, None, 'tensor'), may hold values from -0.0625 to 0.0625
- prior_b_factors: float32 [4, 2, 15360, 64], P(None, None, ('tensor', 'dp')), may hold values from -2 to 2
- first_moment_owned: float32 [4, 2, 15360, 64], P(None, None, ('tensor', 'dp')), may hold values from -6 to 6
- second_moment_owned: float32 [4, 2, 15360, 64], P(None, None, ('tensor', 'dp')), may hold values from 0.5 to 8
- replica_gradients: bfloat16 [64, 4, 2, 15360, 64], P('dp', None, None, 'tensor'), may hold values from -16 to 16
- adapter_of_block: int32 [64, 1], replicated, may hold values from 0 to 3
- live_row_count: int32 [64, 1], replicated, may hold values from 32 to 128
- owner_block_table: int32 [64], replicated, may hold values from 0 to 63, each once
Outputs:
- new_b: float32 [4, 2, 15360, 64], P(None, None, ('tensor', 'dp'))
- new_m: float32 [4, 2, 15360, 64], P(None, None, ('tensor', 'dp'))
- new_v: float32 [4, 2, 15360, 64], P(None, None, ('tensor', 'dp'))
- hidden: bfloat16 [8192, 15360], P('dp', 'tensor')
The draws below stay inside these ranges and needn't reach their ends.
All inputs are finite; a program needn't handle non-finite values.
Results may differ from the reference program's by a relative error of at most 0.0067.
Values may be sent and summed in bfloat16 or wider, within the bound.
A program may use at most 128 MiB of HBM per device.

```python
import math
import jax
import jax.numpy as jnp
from jax import lax

MODEL_WIDTH = 8192
FFW = 15360
ADAPTER_RANK = 64
ADAPTER_COUNT = 4
BLOCK = 128
NBLK = 1
ADAM_STEP = 20
ROWS = 8192
FB = 30
N_DP = 64
N_TENSOR = 8


def draw_live_row_count(key, part):
    key = jax.random.fold_in(key, 7)
    first, second = jax.random.split(key)
    total = N_DP * NBLK
    counts = jax.random.randint(first, (total,), BLOCK // 4, BLOCK + 1)
    spot = jax.random.randint(second, (), 0, total - 1)
    places = jnp.arange(total)
    counts = jnp.where(places == spot, BLOCK, jnp.where(places == spot + 1, BLOCK // 4, counts))
    return counts.reshape(N_DP, NBLK).astype(jnp.int32)


def plant(result, key, low, largest):
    place = [jax.random.randint(jax.random.fold_in(key, axis), (), 0, length) for axis, length in enumerate(result.shape)]
    widest = result.shape.index(max(result.shape))
    neighbour = place[:widest] + [(place[widest] + 1) % result.shape[widest]] + place[widest + 1:]
    return result.at[tuple(place)].set(low).at[tuple(neighbour)].set(largest)


def strengthened(array, key, source, target, shards_of, factor):
    owner, partner = [(jnp.arange(array.shape[position]) // (array.shape[position] // shards_of)).reshape([-1 if axis == position else 1 for axis in range(array.ndim)]) for position in (source, target)]
    chosen = jax.random.permutation(key, shards_of)[partner]
    strong = (owner == chosen) | (owner == (partner + shards_of // 2) % shards_of)
    return jnp.where(strong, factor * array, array)


def level_of(rng, extent, cuts, least, high):
    def one(axis_at, parts):
        steps = jax.random.uniform(jax.random.fold_in(jax.random.fold_in(rng, 6), axis_at), (parts,), jnp.float32, least / len(cuts), high / len(cuts))
        return jnp.repeat(jnp.exp(steps), extent[axis_at] // parts).reshape((-1,) + (1,) * (len(extent) - axis_at - 1))

    gain = one(*cuts[0])
    for cut in cuts[1:]:
        gain = gain * one(*cut)
    return gain


def centred(own_key, shape, scale, limit, cuts=(), kind=jnp.bfloat16):
    factor_of = level_of(own_key, shape, cuts, -0.22, 0.18) if cuts else 1.0
    values = jax.random.normal(own_key, shape, jnp.float32) * scale * factor_of
    return jnp.minimum(jnp.maximum(values, -limit), limit).astype(kind)


def gaussian_with(stream_key, dims, scale, most, pieces, heavy, kind=jnp.bfloat16):
    entries = scale * jax.random.normal(stream_key, dims, jnp.float32)
    if pieces:
        entries = entries * level_of(stream_key, dims, pieces, -0.22, 0.18)
    return jnp.clip(strengthened(entries, jax.random.fold_in(stream_key, 3), *heavy), -most, most).astype(kind)


def setup_inputs(seed: int = 0) -> dict:
    seeds = jax.random.split(jax.random.key(seed), 11)
    tokens = centred(seeds[0], (ROWS, MODEL_WIDTH), 1.0, 6.0, ((0, 64), (1, 8)))
    frozen_gate_up = centred(seeds[1], (ROWS, 2, FFW), 1.0, 6.0, ((0, 64), (2, 8)))
    frozen_down_factor = centred(seeds[2], (ADAPTER_COUNT, ADAPTER_RANK, MODEL_WIDTH), MODEL_WIDTH ** -0.5, 0.0625, ((2, 8),))
    prior_b_factors = centred(seeds[3], (ADAPTER_COUNT, 2, FFW, ADAPTER_RANK), 0.125, 2.0, ((2, 512),), jnp.float32)
    first_moment_owned = centred(seeds[4], (ADAPTER_COUNT, 2, FFW, ADAPTER_RANK), 1.0, 6.0, ((2, 512),), jnp.float32)
    second_moment_owned = jnp.clip(jnp.exp(math.log(8.0) - 2.7725887 * jax.random.uniform(seeds[5], (ADAPTER_COUNT, 2, FFW, ADAPTER_RANK), jnp.float32) ** level_of(seeds[5], (ADAPTER_COUNT, 2, FFW, ADAPTER_RANK), ((2, 512),), -0.2, 0.2)), 0.5, 8.0)
    replica_gradients = gaussian_with(seeds[6], (N_DP, ADAPTER_COUNT, 2, FFW, ADAPTER_RANK), 1.0, 16.0, ((0, 64), (3, 8)), (0, 3, 64, 4.0))
    adapter_of_block = plant(jax.random.randint(seeds[7], (N_DP, NBLK), 0, ADAPTER_COUNT), jax.random.fold_in(seeds[7], 1), 0, ADAPTER_COUNT - 1).astype(jnp.int32)
    live_row_count = draw_live_row_count(jax.random.fold_in(seeds[10], 71), 0)
    owner_block_table = jax.random.permutation(seeds[9], N_DP).astype(jnp.int32)
    return dict(tokens=tokens, frozen_gate_up=frozen_gate_up, frozen_down_factor=frozen_down_factor, prior_b_factors=prior_b_factors, first_moment_owned=first_moment_owned, second_moment_owned=second_moment_owned, replica_gradients=replica_gradients, adapter_of_block=adapter_of_block, live_row_count=live_row_count, owner_block_table=owner_block_table)


ADAPTER_SCALE = 2.0
BETA_ONE = 0.9
BETA_TWO = 0.95
LEARN_RATE = 0.05
EPSILON = 1e-08

def owner_inverse(owner_block_table):
    count = owner_block_table.shape[0]
    iota = jnp.arange(count, dtype=jnp.int32)
    return lax.optimization_barrier(jnp.sum(jnp.where(owner_block_table[None, :] == iota[:, None], iota[None, :], 0), axis=1)).astype(jnp.int32)

def reference(tokens, frozen_gate_up, frozen_down_factor, prior_b_factors, first_moment_owned, second_moment_owned, replica_gradients, adapter_of_block, live_row_count, owner_block_table):
    adapters, _, width_ff, rank = prior_b_factors.shape
    inverse = owner_inverse(owner_block_table)
    shaped = prior_b_factors.reshape(adapters, 2, N_TENSOR, N_DP, FB, rank)
    b_natural = shaped[:, :, :, inverse].reshape(adapters, 2, width_ff, rank).astype(jnp.bfloat16)
    grad_sum = lax.optimization_barrier(jnp.sum(replica_gradients.astype(jnp.float32), axis=0))
    grad_total = grad_sum.reshape(adapters, 2, N_TENSOR, N_DP, FB, rank)[:, :, :, owner_block_table].reshape(adapters, 2, width_ff, rank)
    new_m = BETA_ONE * first_moment_owned + (1.0 - BETA_ONE) * grad_total
    new_v = BETA_TWO * second_moment_owned + (1.0 - BETA_TWO) * grad_total * grad_total
    m_hat = new_m / (1.0 - BETA_ONE ** ADAM_STEP)
    v_hat = new_v / (1.0 - BETA_TWO ** ADAM_STEP)
    new_b = prior_b_factors - LEARN_RATE * m_hat / (jnp.sqrt(v_hat) + EPSILON)
    total_blocks = adapter_of_block.shape[0] * adapter_of_block.shape[1]
    row_block = tokens.shape[0] // total_blocks
    grouped_rows = tokens.reshape(total_blocks, row_block, tokens.shape[1])
    base = frozen_gate_up.reshape(total_blocks, row_block, 2, width_ff)
    adapter_labels = adapter_of_block.reshape(-1).astype(jnp.int32)
    counts = live_row_count.reshape(-1).astype(jnp.int32)

    def one_block(items):
        rows_in, frozen_input, adapter_label, count = items
        down_factor = frozen_down_factor[adapter_label]
        shrunk = jnp.dot(rows_in, down_factor.T, preferred_element_type=jnp.float32).astype(jnp.bfloat16)
        factor_b = b_natural[adapter_label]
        adapter_change = jnp.einsum('nr,cgr->ncg', shrunk.astype(jnp.float32), factor_b.astype(jnp.float32))
        gate_up_activations = frozen_input.astype(jnp.float32) + ADAPTER_SCALE * adapter_change
        gated = jax.nn.silu(gate_up_activations[:, 0]) * gate_up_activations[:, 1]
        live = jnp.arange(row_block, dtype=jnp.int32) < count
        return jnp.where(live[:, None], gated, jnp.float32(0.0)).astype(jnp.bfloat16)
    hidden = lax.map(one_block, (grouped_rows, base, adapter_labels, counts)).reshape(tokens.shape[0], width_ff)
    return (new_b, new_m, new_v, hidden)
```

```python
import functools

import jax
import jax.numpy as jnp
from jax import lax
from jax.experimental import pallas as pl
from jax.experimental.pallas import tpu as pltpu
from jax.sharding import PartitionSpec as P

ADAM_STEP = 20


ADAPTER_SCALE = 2.0
BETA_ONE = 0.9
BETA_TWO = 0.95
LEARN_RATE = 0.05
EPSILON = 1e-08

MESH = pl.DeviceIdType.MESH
Z = 16
PLANE = 4
TENSOR = 8
UP = Z // 2 - 1
DOWN = Z // 2
STEPS = Z // 2
FB = 30
PAD = 32
LANES = 128
WIRE = jnp.bfloat16
F32 = jnp.float32
BF16 = jnp.bfloat16


def owner_inverse(owner_block_table):
    count = owner_block_table.shape[0]
    iota = jnp.arange(count, dtype=jnp.int32)
    return jnp.sum(jnp.where(owner_block_table[None, :] == iota[:, None], iota[None, :], 0), axis=1)


def slots_of_batch(step):
    if step == 0:
        return 0, 3
    if step == STEPS - 1:
        return 2 * step + 1, 1
    return 2 * step + 1, 2


def exchange_kernel(
    adapters_ref,
    table_ref,
    inverse_ref,
    tokens_ref,
    down_ref,
    mine_ref,
    grads_ref,
    bt_ref,
    shrunk_ref,
    total_ref,
    own_half,
    other_half,
    terms,
    up_out,
    up_in,
    down_out,
    down_in,
    gather_up,
    gather_down,
    spread_out,
    spread_in,
    final_out,
    final_in,
    partial_sums,
    natural,
    local_sem,
    half_send,
    half_recv,
    up_send,
    up_recv,
    down_send,
    down_recv,
    gup_send,
    gup_recv,
    gdown_send,
    gdown_recv,
    spread_send,
    spread_recv,
    final_send,
    final_recv,
    psum_send,
    psum_recv,
):
    dp = lax.axis_index("dp")
    tensor = lax.axis_index("tensor")
    z = dp // PLANE
    plane = dp % PLANE
    core = plane % 2
    base = z * PLANE
    above = (lax.rem(z + 1, Z) * PLANE + plane, tensor)
    below = (lax.rem(z + Z - 1, Z) * PLANE + plane, tensor)
    sibling = (base + plane - core + (1 - core), tensor)
    mates = [lax.rem(plane + step, PLANE) for step in range(1, PLANE)]
    mate_ids = [(base + mate, tensor) for mate in mates]
    peers = [lax.rem(tensor + step, TENSOR) for step in range(1, TENSOR)]
    peer_ids = [(dp, peer) for peer in peers]

    own_copies = [
        pltpu.make_async_copy(grads_ref.at[2 * core + p], own_half.at[p], local_sem.at[p])
        for p in range(2)
    ]
    for copy in own_copies:
        copy.start()

    barrier = pltpu.get_barrier_semaphore()
    everyone = [above, below] + mate_ids + peer_ids
    for device in everyone:
        pl.semaphore_signal(barrier, inc=1, device_id=device, device_id_type=MESH)

    my_adapter = adapters_ref[dp]
    partial_sums[tensor] = lax.dot_general(
        down_ref[my_adapter],
        tokens_ref[...],
        (((1,), (1,)), ((), ())),
        preferred_element_type=F32,
    )
    plane_adapters = [adapters_ref[base + lax.rem(plane + step, PLANE)] for step in range(PLANE)]

    pl.semaphore_wait(barrier, len(everyone))

    def remote(src, dst, send, recv, device):
        return pltpu.make_async_remote_copy(
            src_ref=src,
            dst_ref=dst,
            send_sem=send,
            recv_sem=recv,
            device_id=device,
            device_id_type=MESH,
        )

    halves = [
        remote(
            grads_ref.at[2 * (1 - core) + p],
            other_half.at[p],
            half_send.at[p],
            half_recv.at[p],
            sibling,
        )
        for p in range(2)
    ]
    for copy in halves:
        copy.start()

    def go_up(step):
        source = mine_ref if step == 0 else gather_up.at[step - 1]
        return remote(source, gather_up.at[step], gup_send.at[step], gup_recv.at[step], above)

    def go_down(step):
        source = mine_ref if step == 0 else gather_down.at[step - 1]
        return remote(source, gather_down.at[step], gdown_send.at[step], gdown_recv.at[step], below)

    gups = [go_up(step) for step in range(DOWN)]
    gdowns = [go_down(step) for step in range(UP)]
    gups[0].start()
    gdowns[0].start()

    psums = [
        remote(
            partial_sums.at[tensor],
            partial_sums.at[tensor],
            psum_send.at[i],
            psum_recv.at[tensor],
            device,
        )
        for i, device in enumerate(peer_ids)
    ]
    for copy in psums:
        copy.start()

    def picker(q):
        window = jnp.minimum((120 * q) // LANES * LANES, 1920 - 2 * LANES)
        offset = 120 * q - window
        row = lax.broadcasted_iota(jnp.int32, (PLANE * PAD, 2 * LANES), 0)
        column = lax.broadcasted_iota(jnp.int32, (PLANE * PAD, 2 * LANES), 1)
        hit = (column == offset + row - 2 * (row // PAD)) & (row % PAD < FB)
        return pl.multiple_of(window, LANES), jnp.where(hit, F32(1.0), F32(0.0)).astype(BF16)

    def turned(half, p, window, pick):
        block = lax.dot_general(
            pick,
            half[p, :, pl.ds(window, 2 * LANES)],
            (((1,), (1,)), ((), ())),
            preferred_element_type=F32,
        )
        return block.reshape(PLANE, PAD, LANES)

    for copy in own_copies:
        copy.wait()

    @pl.loop(0, Z)
    def _(q):
        window, pick = picker(q)
        for p in range(2):
            terms[pl.ds(PLANE * q, PLANE), p] = turned(own_half, p, window, pick)

    for copy in halves:
        copy.wait_recv()

    @pl.loop(0, Z)
    def _(q):
        window, pick = picker(q)
        for p in range(2):
            terms[pl.ds(PLANE * q, PLANE), p] += turned(other_half, p, window, pick)

    def term(target, p, b):
        return terms[table_ref[PLANE * target + b], p]

    def send_up(step, p):
        return remote(
            up_out.at[step, p], up_in.at[step, p], up_send.at[step, p], up_recv.at[step, p], above
        )

    def send_down(step, p):
        return remote(
            down_out.at[step, p],
            down_in.at[step, p],
            down_send.at[step, p],
            down_recv.at[step, p],
            below,
        )

    ups = [[send_up(step, p) for p in range(2)] for step in range(UP)]
    downs = [[send_down(step, p) for p in range(2)] for step in range(DOWN)]

    def spread(step, i):
        first, count = slots_of_batch(step)
        return remote(
            spread_out.at[i, pl.ds(first, count)],
            spread_in.at[plane, pl.ds(first, count)],
            spread_send.at[step, i],
            spread_recv.at[step, plane],
            mate_ids[i],
        )

    def choose(block, adapter):
        result = block[0]
        for a in range(1, 4):
            result = jnp.where(adapter == a, block[a], result)
        return result

    spreads = []
    for step in range(STEPS):
        for p in range(2):
            if step < UP:
                target = lax.rem(z + UP - step, Z)
                if step > 0:
                    ups[step - 1][p].wait_recv()
                for b in range(PLANE):
                    value = term(target, p, b)
                    if step > 0:
                        value = value + up_in[step - 1, p, b].astype(F32)
                    up_out[step, p, b] = value.astype(WIRE)
                ups[step][p].start()
            target = lax.rem(z + Z - DOWN + step, Z)
            if step > 0:
                downs[step - 1][p].wait_recv()
            for b in range(PLANE):
                value = term(target, p, b)
                if step > 0:
                    value = value + down_in[step - 1, p, b].astype(F32)
                down_out[step, p, b] = value.astype(WIRE)
            downs[step][p].start()

        arrived = []
        if step == 0:
            arrived.append(mine_ref[...])
        gups[step].wait_recv()
        if step + 1 < DOWN:
            gups[step + 1].start()
        arrived.append(gather_up[step])
        if step < UP:
            gdowns[step].wait_recv()
            if step + 1 < UP:
                gdowns[step + 1].start()
            arrived.append(gather_down[step])
        first, count = slots_of_batch(step)
        for n in range(count):
            spread_in[plane, first + n] = choose(arrived[n], plane_adapters[0])
            for i in range(PLANE - 1):
                spread_out[i, first + n] = choose(arrived[n], plane_adapters[i + 1])
        for i in range(PLANE - 1):
            copy = spread(step, i)
            copy.start()
            spreads.append(copy)

    for p in range(2):
        ups[UP - 1][p].wait_recv()
        downs[DOWN - 1][p].wait_recv()
        for b in range(PLANE):
            value = (
                term(z, p, b)
                + up_in[UP - 1, p, b].astype(F32)
                + down_in[DOWN - 1, p, b].astype(F32)
            )
            final_out[b, p] = value
    finals = [
        remote(
            final_out.at[mate],
            final_in.at[plane],
            final_send.at[i],
            final_recv.at[plane],
            mate_ids[i],
        )
        for i, mate in enumerate(mates)
    ]
    for copy in finals:
        copy.start()
    final_in[plane] = final_out[plane]

    for peer in peers:
        remote(
            partial_sums.at[peer],
            partial_sums.at[peer],
            psum_send.at[0],
            psum_recv.at[peer],
            peer_ids[0],
        ).wait_recv()
    shrunk = partial_sums[0]
    for i in range(1, TENSOR):
        shrunk = shrunk + partial_sums[i]
    shrunk_ref[...] = shrunk.astype(BF16)

    for step in range(STEPS):
        first, count = slots_of_batch(step)
        for i, mate in enumerate(mates):
            remote(
                spread_out.at[i, pl.ds(first, count)],
                spread_in.at[mate, pl.ds(first, count)],
                spread_send.at[step, i],
                spread_recv.at[step, mate],
                mate_ids[i],
            ).wait_recv()

    @pl.loop(0, Z * PLANE)
    def _(k):
        owner = inverse_ref[k]
        delta = lax.rem(owner // PLANE - z + Z, Z)
        slot = jnp.where(delta < STEPS, 2 * delta, 2 * Z - 1 - 2 * delta)
        natural[k] = spread_in[owner % PLANE, slot]

    @pl.loop(0, 1920 // LANES)
    def _(t):
        first = jnp.minimum((LANES * t) // FB, Z * PLANE - 6)
        offset = LANES * t - FB * first
        row = lax.broadcasted_iota(jnp.int32, (6 * PAD, LANES), 0)
        column = lax.broadcasted_iota(jnp.int32, (6 * PAD, LANES), 1)
        hit = (row - 2 * (row // PAD) == offset + column) & (row % PAD < FB)
        pick = jnp.where(hit, F32(1.0), F32(0.0)).astype(BF16)
        block = lax.dot_general(
            natural[pl.ds(first, 6)].reshape(6 * PAD, LANES),
            pick,
            (((0,), (0,)), ((), ())),
            preferred_element_type=F32,
        )
        bt_ref[:, pl.ds(pl.multiple_of(t * LANES, LANES), LANES)] = block.astype(BF16)

    for i, mate in enumerate(mates):
        remote(
            final_out.at[mate],
            final_in.at[mate],
            final_send.at[i],
            final_recv.at[mate],
            mate_ids[i],
        ).wait_recv()
    for c in range(2):
        for p in range(2):
            total_ref[2 * c + p] = final_in[c, p] + final_in[2 + c, p]

    for copy in halves + gups + gdowns + psums + spreads + finals:
        copy.wait_send()
    for pair in ups + downs:
        for copy in pair:
            copy.wait_send()


def exchange(adapters, table, inverse, tokens, down, mine, grads):
    smem = pl.BlockSpec(memory_space=pltpu.SMEM)
    vmem = pl.BlockSpec(memory_space=pltpu.VMEM)
    dma = pltpu.SemaphoreType.DMA
    chunk = (PLANE, PAD, LANES)
    return pl.pallas_call(
        exchange_kernel,
        out_shape=(
            jax.ShapeDtypeStruct((LANES, 1920), BF16),
            jax.ShapeDtypeStruct((64, 128), BF16),
            jax.ShapeDtypeStruct((4, PAD, LANES), F32),
        ),
        in_specs=[smem, smem, smem, vmem, vmem, vmem, pl.BlockSpec(memory_space=pl.ANY)],
        out_specs=(vmem, vmem, vmem),
        scratch_shapes=[
            pltpu.VMEM((2, LANES, 1920), BF16),
            pltpu.VMEM((2, LANES, 1920), BF16),
            pltpu.VMEM((Z * PLANE, 2, PAD, LANES), F32),
            pltpu.VMEM((UP, 2) + chunk, WIRE),
            pltpu.VMEM((UP, 2) + chunk, WIRE),
            pltpu.VMEM((DOWN, 2) + chunk, WIRE),
            pltpu.VMEM((DOWN, 2) + chunk, WIRE),
            pltpu.VMEM((DOWN, 4, PAD, LANES), BF16),
            pltpu.VMEM((UP, 4, PAD, LANES), BF16),
            pltpu.VMEM((PLANE - 1, Z, PAD, LANES), BF16),
            pltpu.VMEM((PLANE, Z, PAD, LANES), BF16),
            pltpu.VMEM((PLANE, 2, PAD, LANES), F32),
            pltpu.VMEM((PLANE, 2, PAD, LANES), F32),
            pltpu.VMEM((TENSOR, 64, 128), F32),
            pltpu.VMEM((Z * PLANE, PAD, LANES), BF16),
            dma((2,)),
            dma((2,)),
            dma((2,)),
            dma((UP, 2)),
            dma((UP, 2)),
            dma((DOWN, 2)),
            dma((DOWN, 2)),
            dma((DOWN,)),
            dma((DOWN,)),
            dma((UP,)),
            dma((UP,)),
            dma((STEPS, PLANE - 1)),
            dma((STEPS, PLANE)),
            dma((PLANE - 1,)),
            dma((PLANE,)),
            dma((TENSOR - 1,)),
            dma((TENSOR,)),
        ],
        compiler_params=pltpu.CompilerParams(
            collective_id=0,
            has_side_effects=True,
            vmem_limit_bytes=40 * 1024 * 1024,
        ),
        cost_estimate=pl.CostEstimate(
            flops=2_000_000_000, bytes_accessed=8_000_000, transcendentals=0
        ),
        name="exchange",
    )(adapters, table, inverse, tokens, down, mine, grads)


def on_device(
    tokens,
    frozen_gate_up,
    frozen_down_factor,
    prior_b_factors,
    first_moment_owned,
    second_moment_owned,
    replica_gradients,
    adapter_of_block,
    live_row_count,
    owner_block_table,
):
    my_index = lax.axis_index("dp")
    adapters, _, owned_rows, rank = prior_b_factors.shape
    width = replica_gradients.shape[3]
    inverse = owner_inverse(owner_block_table)
    mine = (
        prior_b_factors.astype(BF16)
        .transpose(0, 2, 1, 3)
        .reshape(adapters, owned_rows, 2 * rank)
    )
    mine = jnp.pad(mine, ((0, 0), (0, PAD - owned_rows), (0, 0)))
    grads = (
        replica_gradients.reshape(adapters, 2, width, rank)
        .transpose(0, 1, 3, 2)
        .reshape(adapters, 2 * rank, width)
    )
    chosen, shrunk, total = exchange(
        adapter_of_block.reshape(-1),
        owner_block_table,
        inverse,
        tokens,
        frozen_down_factor,
        mine,
        grads,
    )
    grad_total = (
        total[:, :owned_rows].reshape(adapters, owned_rows, 2, rank).transpose(0, 2, 1, 3)
    )
    adapter_change = jnp.einsum(
        "rn,crg->ncg", shrunk, chosen.reshape(2, rank, width), preferred_element_type=F32
    )
    count = lax.dynamic_index_in_dim(live_row_count, my_index, 0, keepdims=False)
    pre = frozen_gate_up.astype(F32) + ADAPTER_SCALE * adapter_change
    gated = jax.nn.silu(pre[:, 0]) * pre[:, 1]
    live = jnp.arange(tokens.shape[0], dtype=jnp.int32) < count
    hidden = jnp.where(live[:, None], gated, F32(0.0)).astype(BF16)
    new_m = BETA_ONE * first_moment_owned + (1.0 - BETA_ONE) * grad_total
    new_v = BETA_TWO * second_moment_owned + (1.0 - BETA_TWO) * grad_total * grad_total
    m_hat = new_m / (1.0 - BETA_ONE**ADAM_STEP)
    v_hat = new_v / (1.0 - BETA_TWO**ADAM_STEP)
    new_b = prior_b_factors - LEARN_RATE * m_hat / (jnp.sqrt(v_hat) + EPSILON)
    return (new_b, new_m, new_v, hidden)


def solution(mesh):
    placed = (
        P("dp", "tensor"),
        P("dp", None, "tensor"),
        P(None, None, "tensor"),
        P(None, None, ("tensor", "dp"), None),
        P(None, None, ("tensor", "dp"), None),
        P(None, None, ("tensor", "dp"), None),
        P("dp", None, None, "tensor", None),
        P(),
        P(),
        P(),
    )
    return jax.shard_map(
        on_device,
        mesh=mesh,
        in_specs=placed,
        out_specs=(
            P(None, None, ("tensor", "dp"), None),
            P(None, None, ("tensor", "dp"), None),
            P(None, None, ("tensor", "dp"), None),
            P("dp", "tensor"),
        ),
        check_vma=False,
    )
```

```python
import functools

import jax
import jax.numpy as jnp
from jax import lax
from jax.experimental import pallas as pl
from jax.experimental.pallas import tpu as pltpu
from jax.sharding import PartitionSpec as P

ADAM_STEP = 20


ADAPTER_SCALE = 2.0
BETA_ONE = 0.9
BETA_TWO = 0.95
LEARN_RATE = 0.05
EPSILON = 1e-08

MESH = pl.DeviceIdType.MESH
Z = 16
PLANE = 4
TENSOR = 8
UP = Z // 2 - 1
DOWN = Z // 2
STEPS = Z // 2
FB = 30
PAD = 32
LANES = 128
WIRE = jnp.bfloat16
VMEM_LIMIT = 60 * 1024 * 1024
F32 = jnp.float32
BF16 = jnp.bfloat16


def slots_of_batch(step):
    if step == 0:
        return 0, 3
    if step == STEPS - 1:
        return 2 * step + 1, 1
    return 2 * step + 1, 2


def exchange_kernel(
    adapters_ref,
    table_ref,
    counts_ref,
    table_row_ref,
    tokens_ref,
    down_ref,
    prior_ref,
    grads_ref,
    bt_ref,
    shrunk_ref,
    live_ref,
    total_ref,
    tokens_in,
    down_in_all,
    prior_in,
    wide,
    mine,
    inverse_row,
    inverse,
    own_half,
    other_half,
    own_terms,
    other_terms,
    core_out,
    core_in,
    staged,
    up_out,
    up_in,
    down_out,
    down_in,
    gather_up,
    gather_down,
    spread_out,
    spread_in,
    final_out,
    final_in,
    partial_sums,
    natural,
    local_sem,
    core_send,
    core_recv,
    up_send,
    up_recv,
    down_send,
    down_recv,
    gup_send,
    gup_recv,
    gdown_send,
    gdown_recv,
    spread_send,
    spread_recv,
    final_send,
    final_recv,
    psum_send,
    psum_recv,
):
    dp = lax.axis_index("dp")
    tensor = lax.axis_index("tensor")
    z = dp // PLANE
    plane = dp % PLANE
    core = plane % 2
    base = z * PLANE
    above = (lax.rem(z + 1, Z) * PLANE + plane, tensor)
    below = (lax.rem(z + Z - 1, Z) * PLANE + plane, tensor)
    sibling = (base + plane - core + (1 - core), tensor)
    mates = [lax.rem(plane + step, PLANE) for step in range(1, PLANE)]
    mate_ids = [(base + mate, tensor) for mate in mates]
    peers = [lax.rem(tensor + step, TENSOR) for step in range(1, TENSOR)]
    peer_ids = [(dp, peer) for peer in peers]

    barrier = pltpu.get_barrier_semaphore()
    everyone = [above, below] + mate_ids + peer_ids
    for device in everyone:
        pl.semaphore_signal(barrier, inc=1, device_id=device, device_id_type=MESH)

    def local(src, dst, i):
        copy = pltpu.make_async_copy(src, dst, local_sem.at[i])
        copy.start()
        return copy

    get_prior = local(prior_ref, prior_in, 0)
    get_other = local(grads_ref.at[pl.ds(2 * (1 - core), 2)], other_half, 1)
    get_own = local(grads_ref.at[pl.ds(2 * core, 2)], own_half, 2)
    get_down = local(down_ref, down_in_all, 3)
    get_tokens = local(tokens_ref, tokens_in, 4)

    wide[...] = jnp.zeros_like(wide)
    row = lax.broadcasted_iota(jnp.int32, (64, 64), 0)
    column = lax.broadcasted_iota(jnp.int32, (64, 64), 1)
    table_rows = jnp.broadcast_to(table_row_ref[...], (64, 64))
    table_column = jnp.sum(jnp.where(row == column, table_rows, 0), axis=1, keepdims=True)
    inverse_row[...] = jnp.sum(jnp.where(table_column == column, row, 0), axis=0, keepdims=True)
    get_inverse = local(inverse_row, inverse, 5)

    get_prior.wait()
    for a in range(4):
        for c in range(2):
            wide[a, pl.ds(0, FB), pl.ds(64 * c, 64)] = prior_in[
                pl.ds(2 * FB * a + c, FB, stride=2), :
            ]
    mine[...] = wide[...].astype(BF16)

    def picker(q):
        window = jnp.minimum((120 * q) // LANES * LANES, 1920 - 2 * LANES)
        offset = 120 * q - window
        row = lax.broadcasted_iota(jnp.int32, (PLANE * PAD, 2 * LANES), 0)
        column = lax.broadcasted_iota(jnp.int32, (PLANE * PAD, 2 * LANES), 1)
        hit = (column == offset + row - 2 * (row // PAD)) & (row % PAD < FB)
        return pl.multiple_of(window, LANES), jnp.where(hit, F32(1.0), F32(0.0)).astype(BF16)

    def turn(half, terms):
        @pl.loop(0, Z, unroll=2)
        def _(q):
            window, pick = picker(q)
            for p in range(2):
                block = lax.dot_general(
                    pick,
                    half[p, :, pl.ds(window, 2 * LANES)],
                    (((1,), (1,)), ((), ())),
                    preferred_element_type=F32,
                )
                terms[pl.ds(PLANE * q, PLANE), p] = block.reshape(PLANE, PAD, LANES).astype(BF16)

    get_other.wait()
    turn(other_half, other_terms)

    pl.semaphore_wait(barrier, len(everyone))

    def remote(src, dst, send, recv, device):
        return pltpu.make_async_remote_copy(
            src_ref=src,
            dst_ref=dst,
            send_sem=send,
            recv_sem=recv,
            device_id=device,
            device_id_type=MESH,
        )

    def go_up(step):
        source = mine if step == 0 else gather_up.at[step - 1]
        return remote(source, gather_up.at[step], gup_send.at[step], gup_recv.at[step], above)

    def go_down(step):
        source = mine if step == 0 else gather_down.at[step - 1]
        return remote(source, gather_down.at[step], gdown_send.at[step], gdown_recv.at[step], below)

    gups = [go_up(step) for step in range(DOWN)]
    gdowns = [go_down(step) for step in range(UP)]
    gups[0].start()
    gdowns[0].start()

    def target_of(way, step):
        if way == 0:
            return lax.rem(z + UP - step, Z)
        return lax.rem(z + Z - DOWN + step, Z)

    def chunk_of(way, step):
        return 2 * step + way

    core_copies = [
        remote(core_out.at[n], core_in.at[n], core_send.at[n], core_recv.at[n], sibling)
        for n in range(2 * STEPS)
    ]

    def serve(step):
        for way in range(2):
            n = chunk_of(way, step)
            target = z if way == 0 and step == UP else target_of(way, step)
            for b in range(PLANE):
                core_out[n, :, b] = other_terms[table_ref[PLANE * target + b]]
            core_copies[n].start()

    serve(0)
    serve(1)

    get_own.wait()
    turn(own_half, own_terms)

    get_down.wait()
    get_tokens.wait()
    partial_sums[tensor] = lax.dot_general(
        down_in_all[adapters_ref[dp]],
        tokens_in[...],
        (((1,), (1,)), ((), ())),
        preferred_element_type=F32,
    )
    psums = [
        remote(
            partial_sums.at[tensor],
            partial_sums.at[tensor],
            psum_send.at[i],
            psum_recv.at[tensor],
            device,
        )
        for i, device in enumerate(peer_ids)
    ]
    for copy in psums:
        copy.start()
    plane_adapters = [adapters_ref[base + lax.rem(plane + step, PLANE)] for step in range(PLANE)]
    live_ref[...] = (
        lax.broadcasted_iota(jnp.int32, (1, 128), 1) < counts_ref[dp]
    ).astype(jnp.int32)

    def send(way, step, p):
        out, into, send_sem, recv_sem = (
            (up_out, up_in, up_send, up_recv)
            if way == 0
            else (down_out, down_in, down_send, down_recv)
        )
        return remote(
            out.at[step, p],
            into.at[step, p],
            send_sem.at[step, p],
            recv_sem.at[step, p],
            above if way == 0 else below,
        )

    hops = [
        [[send(way, step, p) for p in range(2)] for step in range((UP, DOWN)[way])]
        for way in range(2)
    ]

    def prepare(step):
        for way in range(2):
            n = chunk_of(way, step)
            target = z if way == 0 and step == UP else target_of(way, step)
            core_copies[n].wait_recv()
            for b in range(PLANE):
                staged[way, :, b] = own_terms[table_ref[PLANE * target + b]].astype(F32) + core_in[
                    n, :, b
                ].astype(F32)

    def spread(step, i):
        first, count = slots_of_batch(step)
        return remote(
            spread_out.at[i, pl.ds(first, count)],
            spread_in.at[plane, pl.ds(first, count)],
            spread_send.at[step, i],
            spread_recv.at[step, plane],
            mate_ids[i],
        )

    def choose(block, adapter):
        result = block[0]
        for a in range(1, 4):
            result = jnp.where(adapter == a, block[a], result)
        return result

    spreads = []

    def gather(step):
        arrived = []
        if step == 0:
            arrived.append(mine[...])
        gups[step].wait_recv()
        if step + 1 < DOWN:
            gups[step + 1].start()
        arrived.append(gather_up[step])
        if step < UP:
            gdowns[step].wait_recv()
            if step + 1 < UP:
                gdowns[step + 1].start()
            arrived.append(gather_down[step])
        first, count = slots_of_batch(step)
        for n in range(count):
            spread_in[plane, first + n] = choose(arrived[n], plane_adapters[0])
            for i in range(PLANE - 1):
                spread_out[i, first + n] = choose(arrived[n], plane_adapters[i + 1])
        for i in range(PLANE - 1):
            copy = spread(step, i)
            copy.start()
            spreads.append(copy)

    prepare(0)
    for step in range(STEPS):
        for p in range(2):
            for way in range(2):
                if way == 0 and step == UP:
                    continue
                value = staged[way, p]
                if step > 0:
                    hops[way][step - 1][p].wait_recv()
                    value = value + (up_in, down_in)[way][step - 1, p].astype(F32)
                (up_out, down_out)[way][step, p] = value.astype(WIRE)
                hops[way][step][p].start()
        if step + 2 < STEPS:
            serve(step + 2)
        gather(step)
        if step + 1 < STEPS:
            prepare(step + 1)

    for p in range(2):
        hops[0][UP - 1][p].wait_recv()
        hops[1][DOWN - 1][p].wait_recv()
        final_out[:, p] = (
            staged[0, p] + up_in[UP - 1, p].astype(F32) + down_in[DOWN - 1, p].astype(F32)
        )
    finals = [
        remote(
            final_out.at[mate],
            final_in.at[plane],
            final_send.at[i],
            final_recv.at[plane],
            mate_ids[i],
        )
        for i, mate in enumerate(mates)
    ]
    for copy in finals:
        copy.start()
    final_in[plane] = final_out[plane]

    for peer in peers:
        remote(
            partial_sums.at[peer],
            partial_sums.at[peer],
            psum_send.at[0],
            psum_recv.at[peer],
            peer_ids[0],
        ).wait_recv()
    shrunk = partial_sums[0]
    for i in range(1, TENSOR):
        shrunk = shrunk + partial_sums[i]
    shrunk_ref[...] = shrunk.astype(BF16)

    for step in range(STEPS):
        first, count = slots_of_batch(step)
        for i, mate in enumerate(mates):
            remote(
                spread_out.at[i, pl.ds(first, count)],
                spread_in.at[mate, pl.ds(first, count)],
                spread_send.at[step, i],
                spread_recv.at[step, mate],
                mate_ids[i],
            ).wait_recv()

    get_inverse.wait()

    @pl.loop(0, Z * PLANE, unroll=8)
    def _(k):
        owner = inverse[0, k]
        delta = lax.rem(owner // PLANE - z + Z, Z)
        slot = jnp.where(delta < STEPS, 2 * delta, 2 * Z - 1 - 2 * delta)
        natural[k] = spread_in[owner % PLANE, slot]

    @pl.loop(0, 1920 // LANES, unroll=5)
    def _(t):
        first = jnp.minimum((LANES * t) // FB, Z * PLANE - 6)
        offset = LANES * t - FB * first
        row = lax.broadcasted_iota(jnp.int32, (6 * PAD, LANES), 0)
        column = lax.broadcasted_iota(jnp.int32, (6 * PAD, LANES), 1)
        hit = (row - 2 * (row // PAD) == offset + column) & (row % PAD < FB)
        pick = jnp.where(hit, F32(1.0), F32(0.0)).astype(BF16)
        block = lax.dot_general(
            natural[pl.ds(first, 6)].reshape(6 * PAD, LANES),
            pick,
            (((0,), (0,)), ((), ())),
            preferred_element_type=F32,
        )
        bt_ref[:, pl.ds(pl.multiple_of(t * LANES, LANES), LANES)] = block.astype(BF16)

    for i, mate in enumerate(mates):
        remote(
            final_out.at[mate],
            final_in.at[mate],
            final_send.at[i],
            final_recv.at[mate],
            mate_ids[i],
        ).wait_recv()
    for c in range(2):
        for p in range(2):
            total_ref[2 * c + p] = final_in[c, p] + final_in[2 + c, p]

    for copy in core_copies + gups + gdowns + psums + spreads + finals:
        copy.wait_send()
    for way in hops:
        for pair in way:
            for copy in pair:
                copy.wait_send()


def exchange(adapters, table, counts, tokens, down, prior, grads):
    smem = pl.BlockSpec(memory_space=pltpu.SMEM)
    vmem = pl.BlockSpec(memory_space=pltpu.VMEM)
    hbm = pl.BlockSpec(memory_space=pl.ANY)
    dma = pltpu.SemaphoreType.DMA
    chunk = (PLANE, PAD, LANES)
    return pl.pallas_call(
        exchange_kernel,
        out_shape=(
            jax.ShapeDtypeStruct((LANES, 1920), BF16),
            jax.ShapeDtypeStruct((64, 128), BF16),
            jax.ShapeDtypeStruct((1, 128), jnp.int32),
            jax.ShapeDtypeStruct((4, PAD, LANES), F32),
        ),
        in_specs=[smem, smem, smem, vmem, hbm, hbm, hbm, hbm],
        out_specs=(vmem, vmem, vmem, vmem),
        scratch_shapes=[
            pltpu.VMEM((128, 1024), BF16),
            pltpu.VMEM((4, 64, 1024), BF16),
            pltpu.VMEM((240, 64), F32),
            pltpu.VMEM((4, PAD, LANES), F32),
            pltpu.VMEM((4, PAD, LANES), BF16),
            pltpu.VMEM((1, 64), jnp.int32),
            pltpu.SMEM((1, 64), jnp.int32),
            pltpu.VMEM((2, LANES, 1920), BF16),
            pltpu.VMEM((2, LANES, 1920), BF16),
            pltpu.VMEM((Z * PLANE, 2, PAD, LANES), BF16),
            pltpu.VMEM((Z * PLANE, 2, PAD, LANES), BF16),
            pltpu.VMEM((2 * STEPS, 2) + chunk, BF16),
            pltpu.VMEM((2 * STEPS, 2) + chunk, BF16),
            pltpu.VMEM((2, 2) + chunk, F32),
            pltpu.VMEM((UP, 2) + chunk, WIRE),
            pltpu.VMEM((UP, 2) + chunk, WIRE),
            pltpu.VMEM((DOWN, 2) + chunk, WIRE),
            pltpu.VMEM((DOWN, 2) + chunk, WIRE),
            pltpu.VMEM((DOWN, 4, PAD, LANES), BF16),
            pltpu.VMEM((UP, 4, PAD, LANES), BF16),
            pltpu.VMEM((PLANE - 1, Z, PAD, LANES), BF16),
            pltpu.VMEM((PLANE, Z, PAD, LANES), BF16),
            pltpu.VMEM((PLANE, 2, PAD, LANES), F32),
            pltpu.VMEM((PLANE, 2, PAD, LANES), F32),
            pltpu.VMEM((TENSOR, 64, 128), F32),
            pltpu.VMEM((Z * PLANE, PAD, LANES), BF16),
            dma((6,)),
            dma((2 * STEPS,)),
            dma((2 * STEPS,)),
            dma((UP, 2)),
            dma((UP, 2)),
            dma((DOWN, 2)),
            dma((DOWN, 2)),
            dma((DOWN,)),
            dma((DOWN,)),
            dma((UP,)),
            dma((UP,)),
            dma((STEPS, PLANE - 1)),
            dma((STEPS, PLANE)),
            dma((PLANE - 1,)),
            dma((PLANE,)),
            dma((TENSOR - 1,)),
            dma((TENSOR,)),
        ],
        compiler_params=pltpu.CompilerParams(
            collective_id=0,
            has_side_effects=True,
            vmem_limit_bytes=VMEM_LIMIT,
        ),
        cost_estimate=pl.CostEstimate(
            flops=2_000_000_000, bytes_accessed=8_000_000, transcendentals=0
        ),
        name="exchange",
    )(adapters, table, counts, table.reshape(1, -1), tokens, down, prior, grads)


def adam_kernel(total_ref, prior_ref, first_ref, second_ref, b_ref, m_ref, v_ref):
    for a in range(4):
        for c in range(2):
            grad = total_ref[a, pl.ds(0, FB), pl.ds(64 * c, 64)]
            rows = pl.ds(2 * FB * a + c, FB, stride=2)
            new_m = BETA_ONE * first_ref[rows, :] + (1.0 - BETA_ONE) * grad
            new_v = BETA_TWO * second_ref[rows, :] + (1.0 - BETA_TWO) * grad * grad
            m_hat = new_m / (1.0 - BETA_ONE**ADAM_STEP)
            v_hat = new_v / (1.0 - BETA_TWO**ADAM_STEP)
            b_ref[rows, :] = prior_ref[rows, :] - LEARN_RATE * m_hat / (jnp.sqrt(v_hat) + EPSILON)
            m_ref[rows, :] = new_m
            v_ref[rows, :] = new_v


def adam(total, prior, first, second):
    vmem = pl.BlockSpec(memory_space=pltpu.VMEM)
    return pl.pallas_call(
        adam_kernel,
        out_shape=(jax.ShapeDtypeStruct((240, 64), F32),) * 3,
        in_specs=[vmem] * 4,
        out_specs=(vmem,) * 3,
        name="adam",
    )(total, prior, first, second)


def on_device(
    tokens,
    frozen_gate_up,
    frozen_down_factor,
    prior_b_factors,
    first_moment_owned,
    second_moment_owned,
    replica_gradients,
    adapter_of_block,
    live_row_count,
    owner_block_table,
):
    adapters, _, owned_rows, rank = prior_b_factors.shape
    width = replica_gradients.shape[3]

    def flat(array):
        return array.transpose(0, 2, 1, 3).reshape(adapters * owned_rows * 2, rank)

    def shaped(array):
        return array.reshape(adapters, owned_rows, 2, rank).transpose(0, 2, 1, 3)

    prior = flat(prior_b_factors)
    grads = (
        replica_gradients.reshape(adapters, 2, width, rank)
        .transpose(0, 1, 3, 2)
        .reshape(adapters, 2 * rank, width)
    )
    chosen, shrunk, live, total = exchange(
        adapter_of_block.reshape(-1),
        owner_block_table,
        live_row_count.reshape(-1),
        tokens,
        frozen_down_factor,
        prior,
        grads,
    )
    adapter_change = jnp.einsum(
        "rn,crg->ncg", shrunk, chosen.reshape(2, rank, width), preferred_element_type=F32
    )
    pre = frozen_gate_up.astype(F32) + ADAPTER_SCALE * adapter_change
    gated = jax.nn.silu(pre[:, 0]) * pre[:, 1]
    hidden = jnp.where((live[0] > 0)[:, None], gated, F32(0.0)).astype(BF16)
    new_b, new_m, new_v = adam(total, prior, flat(first_moment_owned), flat(second_moment_owned))
    return (shaped(new_b), shaped(new_m), shaped(new_v), hidden)


def solution(mesh):
    placed = (
        P("dp", "tensor"),
        P("dp", None, "tensor"),
        P(None, None, "tensor"),
        P(None, None, ("tensor", "dp"), None),
        P(None, None, ("tensor", "dp"), None),
        P(None, None, ("tensor", "dp"), None),
        P("dp", None, None, "tensor", None),
        P(),
        P(),
        P(),
    )
    return jax.shard_map(
        on_device,
        mesh=mesh,
        in_specs=placed,
        out_specs=(
            P(None, None, ("tensor", "dp"), None),
            P(None, None, ("tensor", "dp"), None),
            P(None, None, ("tensor", "dp"), None),
            P("dp", "tensor"),
        ),
        check_vma=False,
    )
```

```python
import functools

import jax
import jax.numpy as jnp
from jax import lax
from jax.experimental import pallas as pl
from jax.experimental.pallas import tpu as pltpu
from jax.sharding import PartitionSpec as P

ADAM_STEP = 20


ADAPTER_SCALE = 2.0
BETA_ONE = 0.9
BETA_TWO = 0.95
LEARN_RATE = 0.05
EPSILON = 1e-08

MESH = pl.DeviceIdType.MESH
Z = 16
PLANE = 4
TENSOR = 8
DOWN = Z // 2
STEPS = Z // 2
ROUNDS = Z // 4
FB = 30
PAD = 32
LANES = 128
WIRE = jnp.bfloat16
VMEM_LIMIT = 60 * 1024 * 1024
F32 = jnp.float32
BF16 = jnp.bfloat16


def slots_of_batch(batch):
    return (0, 5) if batch == 0 else (4 * batch + 1, 4 if batch < ROUNDS - 1 else 3)


def exchange_kernel(
    adapters_hbm,
    table_hbm,
    counts_hbm,
    tokens_ref,
    down_ref,
    prior_ref,
    grads_ref,
    bt_ref,
    shrunk_ref,
    live_ref,
    total_ref,
    adapters_ref,
    table_ref,
    counts_ref,
    table_row_ref,
    tokens_in,
    down_in_all,
    prior_in,
    wide,
    mine,
    inverse_row,
    inverse,
    own_half,
    other_half,
    own_terms,
    other_terms,
    core_out,
    core_in,
    y_out,
    y_in,
    hop_out,
    hop_in,
    gathered,
    spread_out,
    spread_in,
    final_out,
    final_in,
    partial_sums,
    natural,
    local_sem,
    core_send,
    core_recv,
    y_send,
    y_recv,
    hop_send,
    hop_recv,
    gather_send,
    gather_recv,
    spread_send,
    spread_recv,
    final_send,
    final_recv,
    psum_send,
    psum_recv,
):
    dp = lax.axis_index("dp")
    tensor = lax.axis_index("tensor")
    z = dp // PLANE
    plane = dp % PLANE
    core = plane % 2
    half = plane // 2
    base = z * PLANE

    def along(distance):
        return (lax.rem(z + Z + distance, Z) * PLANE + plane, tensor)

    above, below = along(1), along(-1)
    sibling = (base + plane - core + (1 - core), tensor)
    across = (base + (1 - half) * 2 + core, tensor)
    mates = [lax.rem(plane + step, PLANE) for step in range(1, PLANE)]
    mate_ids = [(base + mate, tensor) for mate in mates]
    peers = [lax.rem(tensor + step, TENSOR) for step in range(1, TENSOR)]
    peer_ids = [(dp, peer) for peer in peers]

    barrier = pltpu.get_barrier_semaphore()
    everyone = [above, below, along(2), along(-2)] + mate_ids + peer_ids
    for device in everyone:
        pl.semaphore_signal(barrier, inc=1, device_id=device, device_id_type=MESH)

    def local(src, dst, i):
        copy = pltpu.make_async_copy(src, dst, local_sem.at[i])
        copy.start()
        return copy

    get_small = [
        local(adapters_hbm, adapters_ref, 6),
        local(table_hbm, table_ref, 7),
        local(counts_hbm, counts_ref, 8),
        local(table_hbm, table_row_ref, 9),
    ]
    get_prior = local(prior_ref, prior_in, 0)
    get_other = local(grads_ref.at[pl.ds(2 * (1 - core), 2)], other_half, 1)
    get_own = local(grads_ref.at[pl.ds(2 * core, 2)], own_half, 2)
    get_down = local(down_ref, down_in_all, 3)
    get_tokens = local(tokens_ref, tokens_in, 4)

    wide[...] = jnp.zeros_like(wide)
    for copy in get_small:
        copy.wait()
    row = lax.broadcasted_iota(jnp.int32, (64, 64), 0)
    column = lax.broadcasted_iota(jnp.int32, (64, 64), 1)
    table_rows = jnp.broadcast_to(table_row_ref[...].reshape(1, 64), (64, 64))
    table_column = jnp.sum(jnp.where(row == column, table_rows, 0), axis=1, keepdims=True)
    inverse_row[...] = jnp.sum(jnp.where(table_column == column, row, 0), axis=0, keepdims=True)
    get_inverse = local(inverse_row, inverse, 5)

    get_prior.wait()
    for a in range(4):
        for c in range(2):
            wide[a, pl.ds(0, FB), pl.ds(64 * c, 64)] = prior_in[
                pl.ds(2 * FB * a + c, FB, stride=2), :
            ]
    mine[...] = wide[...].astype(BF16)

    def picker(q):
        window = jnp.minimum((120 * q) // LANES * LANES, 1920 - 2 * LANES)
        offset = 120 * q - window
        row = lax.broadcasted_iota(jnp.int32, (PLANE * PAD, 2 * LANES), 0)
        column = lax.broadcasted_iota(jnp.int32, (PLANE * PAD, 2 * LANES), 1)
        hit = (column == offset + row - 2 * (row // PAD)) & (row % PAD < FB)
        return pl.multiple_of(window, LANES), jnp.where(hit, F32(1.0), F32(0.0)).astype(BF16)

    def turn(half, terms):
        @pl.loop(0, Z, unroll=2)
        def _(q):
            window, pick = picker(q)
            for p in range(2):
                block = lax.dot_general(
                    pick,
                    half[p, :, pl.ds(window, 2 * LANES)],
                    (((1,), (1,)), ((), ())),
                    preferred_element_type=F32,
                )
                terms[pl.ds(PLANE * q, PLANE), p] = block.reshape(PLANE, PAD, LANES).astype(BF16)

    get_other.wait()
    turn(other_half, other_terms)

    pl.semaphore_wait(barrier, len(everyone))

    def remote(src, dst, send, recv, device):
        return pltpu.make_async_remote_copy(
            src_ref=src,
            dst_ref=dst,
            send_sem=send,
            recv_sem=recv,
            device_id=device,
            device_id_type=MESH,
        )

    def pass_on(way, r):
        even = r - 1 if r % 2 else r - 2
        return remote(
            gathered.at[way, even - 1] if even else mine,
            gathered.at[way, r - 1],
            gather_send.at[way, r - 1],
            gather_recv.at[way, r - 1],
            along((1 if way == 0 else -1) * (r - even)),
        )

    blocks = {
        (way, r): pass_on(way, r)
        for r in range(1, Z // 2 + 1)
        for way in range(2)
        if (way, r) != (1, Z // 2)
    }

    def pass_round(batch):
        for r in (2 * batch + 2, 2 * batch + 1):
            for way in range(2):
                if (way, r) in blocks:
                    blocks[way, r].start()

    pass_round(0)

    def chunk_of(way, distance):
        return 2 * (Z // 2 - distance) + way if distance else 0

    def owners_of(way, distance):
        return PLANE * lax.rem(z + Z + (distance if way == 0 else -distance), Z)

    groups = [
        [(way, r) for r in (Z // 2 - 2 * k, Z // 2 - 1 - 2 * k) for way in range(2) if (way, r) != (0, Z // 2)]
        for k in range(Z // 4)
    ] + [[(0, 0)]]
    core_copies = [
        remote(core_out.at[n], core_in.at[n], core_send.at[n], core_recv.at[n], sibling)
        for n in range(Z)
    ]
    y_copies = [
        remote(y_out.at[n], y_in.at[n], y_send.at[n], y_recv.at[n], across) for n in range(Z)
    ]

    def serve(group):
        for way, r in groups[group]:
            n, first = chunk_of(way, r), owners_of(way, r)
            for b in range(PLANE):
                core_out[n, :, b] = other_terms[table_ref[first + b]]
            core_copies[n].start()

    def chip_sum(way, r, side):
        n, first = chunk_of(way, r), owners_of(way, r) + 2 * side
        return [
            own_terms[table_ref[first + b]].astype(F32) + core_in[n, :, 2 * side + b].astype(F32)
            for b in range(2)
        ]

    def serve_across(group):
        for way, r in groups[group]:
            n = chunk_of(way, r)
            core_copies[n].wait_recv()
            for b, value in enumerate(chip_sum(way, r, 1 - half)):
                y_out[n, :, b] = value.astype(WIRE)
            y_copies[n].start()

    serve(0)
    serve(1)

    get_own.wait()
    turn(own_half, own_terms)
    serve_across(0)
    serve(2)
    serve_across(1)

    get_down.wait()
    get_tokens.wait()
    partial_sums[tensor] = lax.dot_general(
        down_in_all[adapters_ref[dp]],
        tokens_in[...],
        (((1,), (1,)), ((), ())),
        preferred_element_type=F32,
    )
    psums = [
        remote(
            partial_sums.at[tensor],
            partial_sums.at[tensor],
            psum_send.at[i],
            psum_recv.at[tensor],
            device,
        )
        for i, device in enumerate(peer_ids)
    ]
    for copy in psums:
        copy.start()
    plane_adapters = [adapters_ref[base + lax.rem(plane + step, PLANE)] for step in range(PLANE)]
    live_ref[...] = (
        lax.broadcasted_iota(jnp.int32, (1, 128), 1) < counts_ref[dp]
    ).astype(jnp.int32)

    hops = {
        (way, r): remote(
            hop_out.at[way, r - 1],
            hop_in.at[way, r - 1],
            hop_send.at[way, r - 1],
            hop_recv.at[way, r - 1],
            along((1 if way == 0 else -1) * (1 if r % 2 else 2)),
        )
        for group in groups[:-1]
        for way, r in group
    }

    def plane_sum(way, r):
        n = chunk_of(way, r)
        y_copies[n].wait_recv()
        return [value + y_in[n, :, b].astype(F32) for b, value in enumerate(chip_sum(way, r, half))]

    def arrived_sum(way, r, values):
        for child in (r + 1, r + 2):
            if (way, child) in hops:
                hops[way, child].wait_recv()
                values = [
                    value + hop_in[way, child - 1, :, b].astype(F32)
                    for b, value in enumerate(values)
                ]
        return values

    def send_round(group):
        for way, r in groups[group]:
            values = plane_sum(way, r)
            if r % 2 == 0:
                values = arrived_sum(way, r, values)
            for b, value in enumerate(values):
                hop_out[way, r - 1, :, b] = value.astype(WIRE)
            hops[way, r].start()

    def spread(batch, i, source, mate):
        first, count = slots_of_batch(batch)
        return remote(
            spread_out.at[i, pl.ds(first, count)],
            spread_in.at[source, pl.ds(first, count)],
            spread_send.at[batch, i],
            spread_recv.at[batch, source],
            mate,
        )

    def choose(block, adapter):
        result = block[0]
        for a in range(1, 4):
            result = jnp.where(adapter == a, block[a], result)
        return result

    spreads = []

    def place(block, slot):
        spread_in[plane, slot] = choose(block, plane_adapters[0])
        for i in range(PLANE - 1):
            spread_out[i, slot] = choose(block, plane_adapters[i + 1])

    def gather(batch):
        for way in range(2):
            if (way, 2 * batch + 2) in blocks:
                blocks[way, 2 * batch + 2].wait_recv()
        if batch + 1 < ROUNDS:
            pass_round(batch + 1)
        if batch == 0:
            place(mine[...], 0)
        for r in (2 * batch + 1, 2 * batch + 2):
            for way in range(2):
                if (way, r) in blocks:
                    if r % 2:
                        blocks[way, r].wait_recv()
                    place(gathered[way, r - 1], 2 * r - 1 + way)
        for i in range(PLANE - 1):
            copy = spread(batch, i, plane, mate_ids[i])
            copy.start()
            spreads.append(copy)

    gather(0)
    serve(3)
    serve(4)
    serve_across(2)
    send_round(0)
    serve_across(3)
    serve_across(4)
    gather(1)
    send_round(1)
    gather(2)
    send_round(2)
    gather(3)
    send_round(3)

    values = plane_sum(0, 0)
    for way in range(2):
        values = arrived_sum(way, 0, values)
    for b, value in enumerate(values):
        final_out[b] = value
    final = remote(
        final_out.at[1 - core], final_in, final_send.at[0], final_recv.at[0], sibling
    )
    final.start()

    for peer in peers:
        remote(
            partial_sums.at[peer],
            partial_sums.at[peer],
            psum_send.at[0],
            psum_recv.at[peer],
            peer_ids[0],
        ).wait_recv()
    shrunk = partial_sums[0]
    for i in range(1, TENSOR):
        shrunk = shrunk + partial_sums[i]
    shrunk_ref[...] = shrunk.astype(BF16)

    for batch in range(ROUNDS):
        for i, mate in enumerate(mates):
            spread(batch, i, mate, mate_ids[i]).wait_recv()

    get_inverse.wait()

    @pl.loop(0, Z * PLANE, unroll=8)
    def _(k):
        owner = inverse[0, k]
        delta = lax.rem(owner // PLANE - z + Z, Z)
        slot = jnp.where(delta < STEPS, 2 * delta, 2 * Z - 1 - 2 * delta)
        natural[k] = spread_in[owner % PLANE, slot]

    @pl.loop(0, 1920 // LANES, unroll=5)
    def _(t):
        first = jnp.minimum((LANES * t) // FB, Z * PLANE - 6)
        offset = LANES * t - FB * first
        row = lax.broadcasted_iota(jnp.int32, (6 * PAD, LANES), 0)
        column = lax.broadcasted_iota(jnp.int32, (6 * PAD, LANES), 1)
        hit = (row - 2 * (row // PAD) == offset + column) & (row % PAD < FB)
        pick = jnp.where(hit, F32(1.0), F32(0.0)).astype(BF16)
        block = lax.dot_general(
            natural[pl.ds(first, 6)].reshape(6 * PAD, LANES),
            pick,
            (((0,), (0,)), ((), ())),
            preferred_element_type=F32,
        )
        bt_ref[:, pl.ds(pl.multiple_of(t * LANES, LANES), LANES)] = block.astype(BF16)

    total_ref[pl.ds(2 * core, 2)] = final_out[core]
    final.wait_recv()
    total_ref[pl.ds(2 * (1 - core), 2)] = final_in[...]

    for copy in core_copies + y_copies + psums + spreads + [final]:
        copy.wait_send()
    for copy in list(hops.values()) + list(blocks.values()):
        copy.wait_send()


def exchange(adapters, table, counts, tokens, down, prior, grads):
    vmem = pl.BlockSpec(memory_space=pltpu.VMEM)
    hbm = pl.BlockSpec(memory_space=pltpu.HBM)
    dma = pltpu.SemaphoreType.DMA
    chunk = (PLANE, PAD, LANES)
    return pl.pallas_call(
        exchange_kernel,
        out_shape=(
            jax.ShapeDtypeStruct((LANES, 1920), BF16),
            jax.ShapeDtypeStruct((64, 128), BF16),
            jax.ShapeDtypeStruct((1, 128), jnp.int32),
            jax.ShapeDtypeStruct((4, PAD, LANES), F32),
        ),
        in_specs=[hbm] * 7,
        out_specs=(vmem, vmem, vmem, vmem),
        scratch_shapes=[
            pltpu.SMEM((64,), jnp.int32),
            pltpu.SMEM((64,), jnp.int32),
            pltpu.SMEM((64,), jnp.int32),
            pltpu.VMEM((64,), jnp.int32),
            pltpu.VMEM((128, 1024), BF16),
            pltpu.VMEM((4, 64, 1024), BF16),
            pltpu.VMEM((240, 64), F32),
            pltpu.VMEM((4, PAD, LANES), F32),
            pltpu.VMEM((4, PAD, LANES), BF16),
            pltpu.VMEM((1, 64), jnp.int32),
            pltpu.SMEM((1, 64), jnp.int32),
            pltpu.VMEM((2, LANES, 1920), BF16),
            pltpu.VMEM((2, LANES, 1920), BF16),
            pltpu.VMEM((Z * PLANE, 2, PAD, LANES), BF16),
            pltpu.VMEM((Z * PLANE, 2, PAD, LANES), BF16),
            pltpu.VMEM((2 * STEPS, 2) + chunk, BF16),
            pltpu.VMEM((2 * STEPS, 2) + chunk, BF16),
            pltpu.VMEM((Z, 2, 2, PAD, LANES), WIRE),
            pltpu.VMEM((Z, 2, 2, PAD, LANES), WIRE),
            pltpu.VMEM((2, DOWN, 2, 2, PAD, LANES), WIRE),
            pltpu.VMEM((2, DOWN, 2, 2, PAD, LANES), WIRE),
            pltpu.VMEM((2, DOWN, 4, PAD, LANES), BF16),
            pltpu.VMEM((PLANE - 1, Z, PAD, LANES), BF16),
            pltpu.VMEM((PLANE, Z, PAD, LANES), BF16),
            pltpu.VMEM((2, 2, PAD, LANES), F32),
            pltpu.VMEM((2, PAD, LANES), F32),
            pltpu.VMEM((TENSOR, 64, 128), F32),
            pltpu.VMEM((Z * PLANE, PAD, LANES), BF16),
            dma((10,)),
            dma((2 * STEPS,)),
            dma((2 * STEPS,)),
            dma((Z,)),
            dma((Z,)),
            dma((2, DOWN)),
            dma((2, DOWN)),
            dma((2, DOWN)),
            dma((2, DOWN)),
            dma((ROUNDS, PLANE - 1)),
            dma((ROUNDS, PLANE)),
            dma((1,)),
            dma((1,)),
            dma((TENSOR - 1,)),
            dma((TENSOR,)),
        ],
        compiler_params=pltpu.CompilerParams(
            collective_id=0,
            has_side_effects=True,
            vmem_limit_bytes=VMEM_LIMIT,
        ),
        cost_estimate=pl.CostEstimate(
            flops=2_000_000_000, bytes_accessed=8_000_000, transcendentals=0
        ),
        name="exchange",
    )(adapters, table, counts, tokens, down, prior, grads)


def adam_kernel(total_ref, prior_ref, first_ref, second_ref, b_ref, m_ref, v_ref):
    for a in range(4):
        for c in range(2):
            grad = total_ref[a, pl.ds(0, FB), pl.ds(64 * c, 64)]
            rows = pl.ds(2 * FB * a + c, FB, stride=2)
            new_m = BETA_ONE * first_ref[rows, :] + (1.0 - BETA_ONE) * grad
            new_v = BETA_TWO * second_ref[rows, :] + (1.0 - BETA_TWO) * grad * grad
            m_hat = new_m / (1.0 - BETA_ONE**ADAM_STEP)
            v_hat = new_v / (1.0 - BETA_TWO**ADAM_STEP)
            b_ref[rows, :] = prior_ref[rows, :] - LEARN_RATE * m_hat / (jnp.sqrt(v_hat) + EPSILON)
            m_ref[rows, :] = new_m
            v_ref[rows, :] = new_v


def adam(total, prior, first, second):
    vmem = pl.BlockSpec(memory_space=pltpu.VMEM)
    return pl.pallas_call(
        adam_kernel,
        out_shape=(jax.ShapeDtypeStruct((240, 64), F32),) * 3,
        in_specs=[vmem] * 4,
        out_specs=(vmem,) * 3,
        name="adam",
    )(total, prior, first, second)


def on_device(
    tokens,
    frozen_gate_up,
    frozen_down_factor,
    prior_b_factors,
    first_moment_owned,
    second_moment_owned,
    replica_gradients,
    adapter_of_block,
    live_row_count,
    owner_block_table,
):
    adapters, _, owned_rows, rank = prior_b_factors.shape
    width = replica_gradients.shape[3]

    def flat(array):
        return array.transpose(0, 2, 1, 3).reshape(adapters * owned_rows * 2, rank)

    def shaped(array):
        return array.reshape(adapters, owned_rows, 2, rank).transpose(0, 2, 1, 3)

    prior = flat(prior_b_factors)
    grads = (
        replica_gradients.reshape(adapters, 2, width, rank)
        .transpose(0, 1, 3, 2)
        .reshape(adapters, 2 * rank, width)
    )
    chosen, shrunk, live, total = exchange(
        adapter_of_block.reshape(-1),
        owner_block_table,
        live_row_count.reshape(-1),
        tokens,
        frozen_down_factor,
        prior,
        grads,
    )
    adapter_change = jnp.einsum(
        "rn,crg->ncg", shrunk, chosen.reshape(2, rank, width), preferred_element_type=F32
    )
    pre = frozen_gate_up.astype(F32) + ADAPTER_SCALE * adapter_change
    gated = jax.nn.silu(pre[:, 0]) * pre[:, 1]
    hidden = jnp.where((live[0] > 0)[:, None], gated, F32(0.0)).astype(BF16)
    new_b, new_m, new_v = adam(total, prior, flat(first_moment_owned), flat(second_moment_owned))
    return (shaped(new_b), shaped(new_m), shaped(new_v), hidden)


def solution(mesh):
    placed = (
        P("dp", "tensor"),
        P("dp", None, "tensor"),
        P(None, None, "tensor"),
        P(None, None, ("tensor", "dp"), None),
        P(None, None, ("tensor", "dp"), None),
        P(None, None, ("tensor", "dp"), None),
        P("dp", None, None, "tensor", None),
        P(),
        P(),
        P(),
    )
    return jax.shard_map(
        on_device,
        mesh=mesh,
        in_specs=placed,
        out_specs=(
            P(None, None, ("tensor", "dp"), None),
            P(None, None, ("tensor", "dp"), None),
            P(None, None, ("tensor", "dp"), None),
            P("dp", "tensor"),
        ),
        check_vma=False,
    )
```

```python
import functools

import jax
import jax.numpy as jnp
from jax import lax
from jax.experimental import pallas as pl
from jax.experimental.pallas import tpu as pltpu
from jax.sharding import PartitionSpec as P

ADAM_STEP = 20


ADAPTER_SCALE = 2.0
BETA_ONE = 0.9
BETA_TWO = 0.95
LEARN_RATE = 0.05
EPSILON = 1e-08

MESH = pl.DeviceIdType.MESH
Z = 16
PLANE = 4
WIDE = 4
DOWN = Z // 2
STEPS = Z // 2
ROUNDS = Z // 4
FB = 30
PAD = 32
LANES = 128
WIRE = jnp.bfloat16
VMEM_LIMIT = 60 * 1024 * 1024
F32 = jnp.float32
BF16 = jnp.bfloat16


def slots_of_batch(batch):
    return (0, 5) if batch == 0 else (4 * batch + 1, 4 if batch < ROUNDS - 1 else 3)


def exchange_kernel(
    adapters_hbm,
    table_hbm,
    counts_hbm,
    tokens_ref,
    down_ref,
    prior_ref,
    grads_ref,
    bt_ref,
    shrunk_ref,
    live_ref,
    total_ref,
    adapters_ref,
    table_ref,
    counts_ref,
    table_row_ref,
    tokens_in,
    down_in_all,
    prior_in,
    wide,
    mine,
    inverse_row,
    inverse,
    own_half,
    other_half,
    own_terms,
    other_terms,
    core_out,
    core_in,
    y_out,
    y_in,
    early_out,
    early_in,
    hop_out,
    hop_in,
    gathered,
    spread_out,
    spread_in,
    final_out,
    final_in,
    partial_sums,
    pair_sums,
    natural,
    local_sem,
    core_send,
    core_recv,
    y_send,
    y_recv,
    early_send,
    early_recv,
    hop_send,
    hop_recv,
    gather_send,
    gather_recv,
    spread_send,
    spread_recv,
    final_send,
    final_recv,
    pair_send,
    pair_recv,
    psum_send,
    psum_recv,
):
    dp = lax.axis_index("dp")
    tensor = lax.axis_index("tensor")
    z = dp // PLANE
    plane = dp % PLANE
    core = plane % 2
    half = plane // 2
    base = z * PLANE

    def along(distance):
        return (lax.rem(z + Z + distance, Z) * PLANE + plane, tensor)

    above, below = along(1), along(-1)
    sibling = (base + plane - core + (1 - core), tensor)
    across = (base + (1 - half) * 2 + core, tensor)
    mates = [lax.rem(plane + step, PLANE) for step in range(1, PLANE)]
    mate_ids = [(base + mate, tensor) for mate in mates]
    row, place_in_row = tensor // WIDE, tensor % WIDE
    other_row = (dp, (1 - row) * WIDE + place_in_row)
    peers = [lax.rem(place_in_row + step, WIDE) for step in range(1, WIDE)]
    peer_ids = [(dp, row * WIDE + peer) for peer in peers]

    barrier = pltpu.get_barrier_semaphore()
    everyone = [above, below, along(2), along(-2)] + mate_ids + peer_ids + [other_row]
    for device in everyone:
        pl.semaphore_signal(barrier, inc=1, device_id=device, device_id_type=MESH)

    def local(src, dst, i):
        copy = pltpu.make_async_copy(src, dst, local_sem.at[i])
        copy.start()
        return copy

    get_small = [
        local(adapters_hbm, adapters_ref, 6),
        local(table_hbm, table_ref, 7),
        local(counts_hbm, counts_ref, 8),
        local(table_hbm, table_row_ref, 9),
    ]
    get_prior = local(prior_ref, prior_in, 0)
    get_other = local(grads_ref.at[pl.ds(2 * (1 - core), 2)], other_half, 1)
    get_own = local(grads_ref.at[pl.ds(2 * core, 2)], own_half, 2)
    get_down = local(down_ref, down_in_all, 3)
    get_tokens = local(tokens_ref, tokens_in, 4)

    wide[...] = jnp.zeros_like(wide)
    for copy in get_small:
        copy.wait()
    owner_at = lax.broadcasted_iota(jnp.int32, (64, 64), 0)
    block_at = lax.broadcasted_iota(jnp.int32, (64, 64), 1)
    table_rows = jnp.broadcast_to(table_row_ref[...].reshape(1, 64), (64, 64))
    table_column = jnp.sum(jnp.where(owner_at == block_at, table_rows, 0), axis=1, keepdims=True)
    found = jnp.where(table_column == block_at, owner_at, 0)
    inverse_row[...] = jnp.sum(found, axis=0, keepdims=True)
    get_inverse = local(inverse_row, inverse, 5)

    get_prior.wait()
    for a in range(4):
        for c in range(2):
            wide[a, pl.ds(0, FB), pl.ds(64 * c, 64)] = prior_in[
                pl.ds(2 * FB * a + c, FB, stride=2), :
            ]
    mine[...] = wide[...].astype(BF16)

    def picker(q):
        window = jnp.minimum((120 * q) // LANES * LANES, 1920 - 2 * LANES)
        offset = 120 * q - window
        row = lax.broadcasted_iota(jnp.int32, (PLANE * PAD, 2 * LANES), 0)
        column = lax.broadcasted_iota(jnp.int32, (PLANE * PAD, 2 * LANES), 1)
        hit = (column == offset + row - 2 * (row // PAD)) & (row % PAD < FB)
        return pl.multiple_of(window, LANES), jnp.where(hit, F32(1.0), F32(0.0)).astype(BF16)

    def turn(half, terms):
        @pl.loop(0, Z, unroll=2)
        def _(q):
            window, pick = picker(q)
            for p in range(2):
                block = lax.dot_general(
                    pick,
                    half[p, :, pl.ds(window, 2 * LANES)],
                    (((1,), (1,)), ((), ())),
                    preferred_element_type=F32,
                )
                terms[pl.ds(PLANE * q, PLANE), p] = block.reshape(PLANE, PAD, LANES).astype(BF16)

    get_other.wait()
    turn(other_half, other_terms)

    pl.semaphore_wait(barrier, len(everyone))

    def remote(src, dst, send, recv, device):
        return pltpu.make_async_remote_copy(
            src_ref=src,
            dst_ref=dst,
            send_sem=send,
            recv_sem=recv,
            device_id=device,
            device_id_type=MESH,
        )

    def pass_on(way, r):
        even = r - 1 if r % 2 else r - 2
        return remote(
            gathered.at[way, even - 1] if even else mine,
            gathered.at[way, r - 1],
            gather_send.at[way, r - 1],
            gather_recv.at[way, r - 1],
            along((1 if way == 0 else -1) * (r - even)),
        )

    blocks = {
        (way, r): pass_on(way, r)
        for r in range(1, Z // 2 + 1)
        for way in range(2)
        if (way, r) != (1, Z // 2)
    }

    def pass_round(batch):
        for r in (2 * batch + 2, 2 * batch + 1):
            for way in range(2):
                if (way, r) in blocks:
                    blocks[way, r].start()

    pass_round(0)

    def chunk_of(way, distance):
        return 2 * (Z // 2 - distance) + way if distance else 0

    def owners_of(way, distance):
        return PLANE * lax.rem(z + Z + (distance if way == 0 else -distance), Z)

    groups = [
        [(way, r) for r in (Z // 2 - 2 * k, Z // 2 - 1 - 2 * k) for way in range(2) if (way, r) != (0, Z // 2)]
        for k in range(Z // 4)
    ] + [[(0, 0)]]
    core_copies = [
        remote(core_out.at[n], core_in.at[n], core_send.at[n], core_recv.at[n], sibling)
        for n in range(Z)
    ]
    y_copies = [
        remote(y_out.at[n], y_in.at[n], y_send.at[n], y_recv.at[n], across) for n in range(Z)
    ]
    used_y = [y_copies[chunk_of(way, r)] for group in groups[1:] for way, r in group]

    def serve(group):
        for way, r in groups[group]:
            n, first = chunk_of(way, r), owners_of(way, r)
            for b in range(PLANE):
                core_out[n, :, b] = other_terms[table_ref[first + b]]
            core_copies[n].start()

    def chip_sum(way, r, side):
        n, first = chunk_of(way, r), owners_of(way, r) + 2 * side
        return [
            own_terms[table_ref[first + b]].astype(F32) + core_in[n, :, 2 * side + b].astype(F32)
            for b in range(2)
        ]

    early = {
        (way, r): remote(
            early_out.at[way, r - 7],
            early_in.at[way, r - 7],
            early_send.at[way, r - 7],
            early_recv.at[way, r - 7],
            along((1 if way == 0 else -1) * (r - 6)),
        )
        for way, r in groups[0]
    }

    def send_early():
        for way, r in groups[0]:
            core_copies[chunk_of(way, r)].wait_recv()
            for side in range(2):
                for b, value in enumerate(chip_sum(way, r, side)):
                    early_out[way, r - 7, :, 2 * side + b] = value.astype(WIRE)
            early[way, r].start()

    def line_sum(way, r, side):
        values = chip_sum(way, r, side)
        for child in (7, 8) if r == 6 else ():
            if (way, child) in early:
                values = [
                    value + early_in[way, child - 7, :, 2 * side + b].astype(F32)
                    for b, value in enumerate(values)
                ]
        return values

    def serve_across(r):
        for way in range(2 if r else 1):
            n = chunk_of(way, r)
            core_copies[n].wait_recv()
            for child in (7, 8) if r == 6 else ():
                if (way, child) in early:
                    early[way, child].wait_recv()
            for b, value in enumerate(line_sum(way, r, 1 - half)):
                y_out[n, :, b] = value.astype(WIRE)
            y_copies[n].start()

    serve(0)
    serve(1)

    get_own.wait()
    turn(own_half, own_terms)
    send_early()
    serve(2)
    serve_across(5)
    serve_across(4)
    serve(3)
    serve(4)
    serve_across(3)

    get_down.wait()
    get_tokens.wait()
    partial_sums[row] = lax.dot_general(
        down_in_all[adapters_ref[dp]],
        tokens_in[...],
        (((1,), (1,)), ((), ())),
        preferred_element_type=F32,
    )
    pair = remote(
        partial_sums.at[row], partial_sums.at[row], pair_send.at[0], pair_recv.at[row], other_row
    )
    pair.start()

    def psum(i, source):
        return remote(
            pair_sums.at[source],
            pair_sums.at[source],
            psum_send.at[i],
            psum_recv.at[source],
            peer_ids[i],
        )

    psums = [psum(i, place_in_row) for i in range(WIDE - 1)]

    def sum_rows():
        remote(
            partial_sums.at[1 - row],
            partial_sums.at[1 - row],
            pair_send.at[0],
            pair_recv.at[1 - row],
            other_row,
        ).wait_recv()
        pair_sums[place_in_row] = partial_sums[0] + partial_sums[1]
        for copy in psums:
            copy.start()

    plane_adapters = [adapters_ref[base + lax.rem(plane + step, PLANE)] for step in range(PLANE)]
    live_ref[...] = (
        lax.broadcasted_iota(jnp.int32, (1, 128), 1) < counts_ref[dp]
    ).astype(jnp.int32)

    hops = {
        (way, r): remote(
            hop_out.at[way, r - 1],
            hop_in.at[way, r - 1],
            hop_send.at[way, r - 1],
            hop_recv.at[way, r - 1],
            along((1 if way == 0 else -1) * (1 if r % 2 else 2)),
        )
        for group in groups[1:-1]
        for way, r in group
    }

    def plane_sum(way, r):
        n = chunk_of(way, r)
        y_copies[n].wait_recv()
        return [value + y_in[n, :, b].astype(F32) for b, value in enumerate(line_sum(way, r, half))]

    def arrived_sum(way, r, values):
        for child in (r + 1, r + 2):
            if (way, child) in hops:
                hops[way, child].wait_recv()
                values = [
                    value + hop_in[way, child - 1, :, b].astype(F32)
                    for b, value in enumerate(values)
                ]
        return values

    def send_round(group):
        for way, r in groups[group]:
            values = plane_sum(way, r)
            if r % 2 == 0:
                values = arrived_sum(way, r, values)
            for b, value in enumerate(values):
                hop_out[way, r - 1, :, b] = value.astype(WIRE)
            hops[way, r].start()

    def spread(batch, i, source, mate):
        first, count = slots_of_batch(batch)
        return remote(
            spread_out.at[i, pl.ds(first, count)],
            spread_in.at[source, pl.ds(first, count)],
            spread_send.at[batch, i],
            spread_recv.at[batch, source],
            mate,
        )

    def choose(block, adapter):
        result = block[0]
        for a in range(1, 4):
            result = jnp.where(adapter == a, block[a], result)
        return result

    spreads = []

    def place(block, slot):
        spread_in[plane, slot] = choose(block, plane_adapters[0])
        for i in range(PLANE - 1):
            spread_out[i, slot] = choose(block, plane_adapters[i + 1])

    def gather_pass(batch):
        for way in range(2):
            if (way, 2 * batch + 2) in blocks:
                blocks[way, 2 * batch + 2].wait_recv()
        if batch + 1 < ROUNDS:
            pass_round(batch + 1)

    def gather_spread(batch):
        if batch == 0:
            place(mine[...], 0)
        for r in (2 * batch + 1, 2 * batch + 2):
            for way in range(2):
                if (way, r) in blocks:
                    if r % 2:
                        blocks[way, r].wait_recv()
                    place(gathered[way, r - 1], 2 * r - 1 + way)
        for i in range(PLANE - 1):
            copy = spread(batch, i, plane, mate_ids[i])
            copy.start()
            spreads.append(copy)

    gather_pass(0)
    serve_across(6)
    serve_across(2)
    serve_across(1)
    serve_across(0)
    gather_pass(1)
    send_round(1)
    gather_spread(0)
    gather_pass(2)
    gather_spread(1)
    sum_rows()
    send_round(2)
    gather_pass(3)
    gather_spread(2)
    gather_spread(3)
    send_round(3)

    values = plane_sum(0, 0)
    for way in range(2):
        values = arrived_sum(way, 0, values)
    for b, value in enumerate(values):
        final_out[b] = value
    final = remote(
        final_out.at[1 - core], final_in, final_send.at[0], final_recv.at[0], sibling
    )
    final.start()

    for i, peer in enumerate(peers):
        psum(i, peer).wait_recv()
    shrunk = pair_sums[0]
    for i in range(1, WIDE):
        shrunk = shrunk + pair_sums[i]
    shrunk_ref[...] = shrunk.astype(BF16)

    for batch in range(ROUNDS):
        for i, mate in enumerate(mates):
            spread(batch, i, mate, mate_ids[i]).wait_recv()

    get_inverse.wait()

    @pl.loop(0, Z * PLANE, unroll=8)
    def _(k):
        owner = inverse[0, k]
        delta = lax.rem(owner // PLANE - z + Z, Z)
        slot = jnp.where(delta < STEPS, 2 * delta, 2 * Z - 1 - 2 * delta)
        natural[k] = spread_in[owner % PLANE, slot]

    @pl.loop(0, 1920 // LANES, unroll=5)
    def _(t):
        first = jnp.minimum((LANES * t) // FB, Z * PLANE - 6)
        offset = LANES * t - FB * first
        row = lax.broadcasted_iota(jnp.int32, (6 * PAD, LANES), 0)
        column = lax.broadcasted_iota(jnp.int32, (6 * PAD, LANES), 1)
        hit = (row - 2 * (row // PAD) == offset + column) & (row % PAD < FB)
        pick = jnp.where(hit, F32(1.0), F32(0.0)).astype(BF16)
        block = lax.dot_general(
            natural[pl.ds(first, 6)].reshape(6 * PAD, LANES),
            pick,
            (((0,), (0,)), ((), ())),
            preferred_element_type=F32,
        )
        bt_ref[:, pl.ds(pl.multiple_of(t * LANES, LANES), LANES)] = block.astype(BF16)

    total_ref[pl.ds(2 * core, 2)] = final_out[core]
    final.wait_recv()
    total_ref[pl.ds(2 * (1 - core), 2)] = final_in[...]

    for copy in core_copies + used_y + psums + spreads + [pair, final]:
        copy.wait_send()
    for copy in list(early.values()) + list(hops.values()) + list(blocks.values()):
        copy.wait_send()


def exchange(adapters, table, counts, tokens, down, prior, grads):
    vmem = pl.BlockSpec(memory_space=pltpu.VMEM)
    hbm = pl.BlockSpec(memory_space=pltpu.HBM)
    dma = pltpu.SemaphoreType.DMA
    chunk = (PLANE, PAD, LANES)
    return pl.pallas_call(
        exchange_kernel,
        out_shape=(
            jax.ShapeDtypeStruct((LANES, 1920), BF16),
            jax.ShapeDtypeStruct((64, 128), BF16),
            jax.ShapeDtypeStruct((1, 128), jnp.int32),
            jax.ShapeDtypeStruct((4, PAD, LANES), F32),
        ),
        in_specs=[hbm] * 7,
        out_specs=(vmem, vmem, vmem, vmem),
        scratch_shapes=[
            pltpu.SMEM((64,), jnp.int32),
            pltpu.SMEM((64,), jnp.int32),
            pltpu.SMEM((64,), jnp.int32),
            pltpu.VMEM((64,), jnp.int32),
            pltpu.VMEM((128, 1024), BF16),
            pltpu.VMEM((4, 64, 1024), BF16),
            pltpu.VMEM((240, 64), F32),
            pltpu.VMEM((4, PAD, LANES), F32),
            pltpu.VMEM((4, PAD, LANES), BF16),
            pltpu.VMEM((1, 64), jnp.int32),
            pltpu.SMEM((1, 64), jnp.int32),
            pltpu.VMEM((2, LANES, 1920), BF16),
            pltpu.VMEM((2, LANES, 1920), BF16),
            pltpu.VMEM((Z * PLANE, 2, PAD, LANES), BF16),
            pltpu.VMEM((Z * PLANE, 2, PAD, LANES), BF16),
            pltpu.VMEM((2 * STEPS, 2) + chunk, BF16),
            pltpu.VMEM((2 * STEPS, 2) + chunk, BF16),
            pltpu.VMEM((Z, 2, 2, PAD, LANES), WIRE),
            pltpu.VMEM((Z, 2, 2, PAD, LANES), WIRE),
            pltpu.VMEM((2, 2) + (2,) + chunk, WIRE),
            pltpu.VMEM((2, 2) + (2,) + chunk, WIRE),
            pltpu.VMEM((2, DOWN, 2, 2, PAD, LANES), WIRE),
            pltpu.VMEM((2, DOWN, 2, 2, PAD, LANES), WIRE),
            pltpu.VMEM((2, DOWN, 4, PAD, LANES), BF16),
            pltpu.VMEM((PLANE - 1, Z, PAD, LANES), BF16),
            pltpu.VMEM((PLANE, Z, PAD, LANES), BF16),
            pltpu.VMEM((2, 2, PAD, LANES), F32),
            pltpu.VMEM((2, PAD, LANES), F32),
            pltpu.VMEM((2, 64, 128), F32),
            pltpu.VMEM((WIDE, 64, 128), F32),
            pltpu.VMEM((Z * PLANE, PAD, LANES), BF16),
            dma((10,)),
            dma((2 * STEPS,)),
            dma((2 * STEPS,)),
            dma((Z,)),
            dma((Z,)),
            dma((2, 2)),
            dma((2, 2)),
            dma((2, DOWN)),
            dma((2, DOWN)),
            dma((2, DOWN)),
            dma((2, DOWN)),
            dma((ROUNDS, PLANE - 1)),
            dma((ROUNDS, PLANE)),
            dma((1,)),
            dma((1,)),
            dma((1,)),
            dma((2,)),
            dma((WIDE - 1,)),
            dma((WIDE,)),
        ],
        compiler_params=pltpu.CompilerParams(
            collective_id=0,
            has_side_effects=True,
            vmem_limit_bytes=VMEM_LIMIT,
        ),
        cost_estimate=pl.CostEstimate(
            flops=2_000_000_000, bytes_accessed=8_000_000, transcendentals=0
        ),
        name="exchange",
    )(adapters, table, counts, tokens, down, prior, grads)


def adam_kernel(total_ref, prior_ref, first_ref, second_ref, b_ref, m_ref, v_ref):
    for a in range(4):
        for c in range(2):
            grad = total_ref[a, pl.ds(0, FB), pl.ds(64 * c, 64)]
            rows = pl.ds(2 * FB * a + c, FB, stride=2)
            new_m = BETA_ONE * first_ref[rows, :] + (1.0 - BETA_ONE) * grad
            new_v = BETA_TWO * second_ref[rows, :] + (1.0 - BETA_TWO) * grad * grad
            m_hat = new_m / (1.0 - BETA_ONE**ADAM_STEP)
            v_hat = new_v / (1.0 - BETA_TWO**ADAM_STEP)
            b_ref[rows, :] = prior_ref[rows, :] - LEARN_RATE * m_hat / (jnp.sqrt(v_hat) + EPSILON)
            m_ref[rows, :] = new_m
            v_ref[rows, :] = new_v


def adam(total, prior, first, second):
    vmem = pl.BlockSpec(memory_space=pltpu.VMEM)
    return pl.pallas_call(
        adam_kernel,
        out_shape=(jax.ShapeDtypeStruct((240, 64), F32),) * 3,
        in_specs=[vmem] * 4,
        out_specs=(vmem,) * 3,
        name="adam",
    )(total, prior, first, second)


def on_device(
    tokens,
    frozen_gate_up,
    frozen_down_factor,
    prior_b_factors,
    first_moment_owned,
    second_moment_owned,
    replica_gradients,
    adapter_of_block,
    live_row_count,
    owner_block_table,
):
    adapters, _, owned_rows, rank = prior_b_factors.shape
    width = replica_gradients.shape[3]

    def flat(array):
        return array.transpose(0, 2, 1, 3).reshape(adapters * owned_rows * 2, rank)

    def shaped(array):
        return array.reshape(adapters, owned_rows, 2, rank).transpose(0, 2, 1, 3)

    prior = flat(prior_b_factors)
    grads = (
        replica_gradients.reshape(adapters, 2, width, rank)
        .transpose(0, 1, 3, 2)
        .reshape(adapters, 2 * rank, width)
    )
    chosen, shrunk, live, total = exchange(
        adapter_of_block.reshape(-1),
        owner_block_table,
        live_row_count.reshape(-1),
        tokens,
        frozen_down_factor,
        prior,
        grads,
    )
    adapter_change = jnp.einsum(
        "rn,crg->ncg", shrunk, chosen.reshape(2, rank, width), preferred_element_type=F32
    )
    pre = frozen_gate_up.astype(F32) + ADAPTER_SCALE * adapter_change
    gated = jax.nn.silu(pre[:, 0]) * pre[:, 1]
    hidden = jnp.where((live[0] > 0)[:, None], gated, F32(0.0)).astype(BF16)
    new_b, new_m, new_v = adam(total, prior, flat(first_moment_owned), flat(second_moment_owned))
    return (shaped(new_b), shaped(new_m), shaped(new_v), hidden)


def solution(mesh):
    placed = (
        P("dp", "tensor"),
        P("dp", None, "tensor"),
        P(None, None, "tensor"),
        P(None, None, ("tensor", "dp"), None),
        P(None, None, ("tensor", "dp"), None),
        P(None, None, ("tensor", "dp"), None),
        P("dp", None, None, "tensor", None),
        P(),
        P(),
        P(),
    )
    return jax.shard_map(
        on_device,
        mesh=mesh,
        in_specs=placed,
        out_specs=(
            P(None, None, ("tensor", "dp"), None),
            P(None, None, ("tensor", "dp"), None),
            P(None, None, ("tensor", "dp"), None),
            P("dp", "tensor"),
        ),
        check_vma=False,
    )
```

```python
import functools

import jax
import jax.numpy as jnp
from jax import lax
from jax.experimental import pallas as pl
from jax.experimental.pallas import tpu as pltpu
from jax.sharding import PartitionSpec as P

ADAM_STEP = 20


ADAPTER_SCALE = 2.0
BETA_ONE = 0.9
BETA_TWO = 0.95
LEARN_RATE = 0.05
EPSILON = 1e-08

MESH = pl.DeviceIdType.MESH
Z = 16
PLANE = 4
WIDE = 4
DOWN = Z // 2
STEPS = Z // 2
ROUNDS = Z // 4
FB = 30
PAD = 32
LANES = 128
WIRE = jnp.bfloat16
VMEM_LIMIT = 60 * 1024 * 1024
F32 = jnp.float32
BF16 = jnp.bfloat16


def slots_of_batch(batch):
    return (0, 5) if batch == 0 else (4 * batch + 1, 4 if batch < ROUNDS - 1 else 3)


def exchange_kernel(
    adapters_hbm,
    table_hbm,
    counts_hbm,
    tokens_ref,
    down_ref,
    prior_ref,
    grads_ref,
    bt_ref,
    shrunk_ref,
    live_ref,
    total_ref,
    adapters_ref,
    table_ref,
    counts_ref,
    table_row_ref,
    tokens_in,
    down_in_all,
    prior_in,
    wide,
    mine,
    lag,
    inverse_row,
    inverse,
    own_half,
    other_half,
    own_terms,
    other_terms,
    core_out,
    core_in,
    y_out,
    y_in,
    early_out,
    early_in,
    hop_out,
    hop_in,
    gathered,
    spread_out,
    spread_in,
    final_out,
    final_in,
    partial_sums,
    pair_sums,
    natural,
    factor,
    local_sem,
    core_send,
    core_recv,
    y_send,
    y_recv,
    early_send,
    early_recv,
    hop_send,
    hop_recv,
    gather_send,
    gather_recv,
    spread_send,
    spread_recv,
    final_send,
    final_recv,
    pair_send,
    pair_recv,
    psum_send,
    psum_recv,
):
    dp = lax.axis_index("dp")
    tensor = lax.axis_index("tensor")
    z = dp // PLANE
    plane = dp % PLANE
    core = plane % 2
    half = plane // 2
    base = z * PLANE

    def along(distance):
        return (lax.rem(z + Z + distance, Z) * PLANE + plane, tensor)

    above, below = along(1), along(-1)
    sibling = (base + plane - core + (1 - core), tensor)
    across = (base + (1 - half) * 2 + core, tensor)
    mates = [lax.rem(plane + step, PLANE) for step in range(1, PLANE)]
    mate_ids = [(base + mate, tensor) for mate in mates]
    row, place_in_row = tensor // WIDE, tensor % WIDE
    other_row = (dp, (1 - row) * WIDE + place_in_row)
    peers = [lax.rem(place_in_row + step, WIDE) for step in range(1, WIDE)]
    peer_ids = [(dp, row * WIDE + peer) for peer in peers]

    barrier = pltpu.get_barrier_semaphore()
    everyone = [above, below, along(2), along(-2)] + mate_ids + peer_ids + [other_row]
    for device in everyone:
        pl.semaphore_signal(barrier, inc=1, device_id=device, device_id_type=MESH)

    def local(src, dst, i):
        copy = pltpu.make_async_copy(src, dst, local_sem.at[i])
        copy.start()
        return copy

    get_small = [
        local(adapters_hbm, adapters_ref, 6),
        local(table_hbm, table_ref, 7),
        local(counts_hbm, counts_ref, 8),
        local(table_hbm, table_row_ref, 9),
    ]
    get_prior = local(prior_ref, prior_in, 0)
    get_other = local(grads_ref.at[pl.ds(2 * (1 - core), 2)], other_half, 1)
    get_own = local(grads_ref.at[pl.ds(2 * core, 2)], own_half, 2)
    get_down = local(down_ref, down_in_all, 3)
    get_tokens = local(tokens_ref, tokens_in, 4)

    wide[...] = jnp.zeros_like(wide)
    for copy in get_small:
        copy.wait()
    owner_at = lax.broadcasted_iota(jnp.int32, (64, 64), 0)
    block_at = lax.broadcasted_iota(jnp.int32, (64, 64), 1)
    table_rows = jnp.broadcast_to(table_row_ref[...].reshape(1, 64), (64, 64))
    table_column = jnp.sum(jnp.where(owner_at == block_at, table_rows, 0), axis=1, keepdims=True)
    found = jnp.where(table_column == block_at, owner_at, 0)
    inverse_row[...] = jnp.sum(found, axis=0, keepdims=True)
    get_inverse = local(inverse_row, inverse, 5)

    get_prior.wait()
    for a in range(4):
        for c in range(2):
            wide[a, pl.ds(0, FB), pl.ds(64 * c, 64)] = prior_in[
                pl.ds(2 * FB * a + c, FB, stride=2), :
            ]
    mine[...] = wide[...].astype(BF16)

    turn_row = lax.broadcasted_iota(jnp.int32, (PLANE * PAD, 2 * LANES), 0)
    turn_column = lax.broadcasted_iota(jnp.int32, (PLANE * PAD, 2 * LANES), 1)
    lag[...] = jnp.where(turn_row % PAD < FB, turn_column - turn_row + 2 * (turn_row // PAD), -1)

    def turn(half, terms):
        @pl.loop(0, Z, unroll=4)
        def _(q):
            window = pl.multiple_of(
                jnp.minimum((120 * q) // LANES * LANES, 1920 - 2 * LANES), LANES
            )
            offset = 120 * q - window
            pick = jnp.where(lag[...] == offset, F32(1.0), F32(0.0)).astype(BF16)
            block = lax.dot_general(
                pick,
                half[:, :, pl.ds(window, 2 * LANES)].reshape(2 * LANES, 2 * LANES),
                (((1,), (1,)), ((), ())),
                preferred_element_type=F32,
            ).astype(BF16)
            for p in range(2):
                terms[pl.ds(PLANE * q, PLANE), p] = block[:, p * LANES : (p + 1) * LANES].reshape(
                    PLANE, PAD, LANES
                )

    get_other.wait()
    turn(other_half, other_terms)

    pl.semaphore_wait(barrier, len(everyone))

    def remote(src, dst, send, recv, device):
        return pltpu.make_async_remote_copy(
            src_ref=src,
            dst_ref=dst,
            send_sem=send,
            recv_sem=recv,
            device_id=device,
            device_id_type=MESH,
        )

    def pass_on(way, r):
        even = r - 1 if r % 2 else r - 2
        return remote(
            gathered.at[way, even - 1] if even else mine,
            gathered.at[way, r - 1],
            gather_send.at[way, r - 1],
            gather_recv.at[way, r - 1],
            along((1 if way == 0 else -1) * (r - even)),
        )

    blocks = {
        (way, r): pass_on(way, r)
        for r in range(1, Z // 2 + 1)
        for way in range(2)
        if (way, r) != (1, Z // 2)
    }

    def pass_round(batch):
        for r in (2 * batch + 2, 2 * batch + 1):
            for way in range(2):
                if (way, r) in blocks:
                    blocks[way, r].start()

    pass_round(0)

    def chunk_of(way, distance):
        return 2 * (Z // 2 - distance) + way if distance else 0

    def owners_of(way, distance):
        return PLANE * lax.rem(z + Z + (distance if way == 0 else -distance), Z)

    groups = [
        [(way, r) for r in (Z // 2 - 2 * k, Z // 2 - 1 - 2 * k) for way in range(2) if (way, r) != (0, Z // 2)]
        for k in range(Z // 4)
    ] + [[(0, 0)]]
    core_copies = [
        remote(core_out.at[n], core_in.at[n], core_send.at[n], core_recv.at[n], sibling)
        for n in range(Z)
    ]
    y_copies = [
        remote(y_out.at[n], y_in.at[n], y_send.at[n], y_recv.at[n], across) for n in range(Z)
    ]
    used_y = [y_copies[chunk_of(way, r)] for group in groups[1:] for way, r in group]

    def serve(group):
        for way, r in groups[group]:
            n, first = chunk_of(way, r), owners_of(way, r)
            for b in range(PLANE):
                core_out[n, :, b] = other_terms[table_ref[first + b]]
            core_copies[n].start()

    def chip_sum(way, r, side):
        n, first = chunk_of(way, r), owners_of(way, r) + 2 * side
        return [
            own_terms[table_ref[first + b]].astype(F32) + core_in[n, :, 2 * side + b].astype(F32)
            for b in range(2)
        ]

    early = {
        (way, r): remote(
            early_out.at[way, r - 7],
            early_in.at[way, r - 7],
            early_send.at[way, r - 7],
            early_recv.at[way, r - 7],
            along((1 if way == 0 else -1) * (r - 6)),
        )
        for way, r in groups[0]
    }

    def send_early():
        for way, r in groups[0]:
            core_copies[chunk_of(way, r)].wait_recv()
            for side in range(2):
                for b, value in enumerate(chip_sum(way, r, side)):
                    early_out[way, r - 7, :, 2 * side + b] = value.astype(WIRE)
            early[way, r].start()

    def line_sum(way, r, side):
        values = chip_sum(way, r, side)
        for child in (7, 8) if r == 6 else ():
            if (way, child) in early:
                values = [
                    value + early_in[way, child - 7, :, 2 * side + b].astype(F32)
                    for b, value in enumerate(values)
                ]
        return values

    def serve_across(r):
        for way in range(2 if r else 1):
            n = chunk_of(way, r)
            core_copies[n].wait_recv()
            for child in (7, 8) if r == 6 else ():
                if (way, child) in early:
                    early[way, child].wait_recv()
            for b, value in enumerate(line_sum(way, r, 1 - half)):
                y_out[n, :, b] = value.astype(WIRE)
            y_copies[n].start()

    serve(0)
    serve(1)

    get_own.wait()
    turn(own_half, own_terms)
    send_early()
    serve(2)
    serve_across(5)
    serve_across(4)
    serve(3)
    serve(4)

    get_down.wait()
    get_tokens.wait()
    partial_sums[row] = lax.dot_general(
        down_in_all[adapters_ref[dp]],
        tokens_in[...],
        (((1,), (1,)), ((), ())),
        preferred_element_type=F32,
    )
    pair = remote(
        partial_sums.at[row], partial_sums.at[row], pair_send.at[0], pair_recv.at[row], other_row
    )
    pair.start()

    def psum(i, source):
        return remote(
            pair_sums.at[source],
            pair_sums.at[source],
            psum_send.at[i],
            psum_recv.at[source],
            peer_ids[i],
        )

    psums = [psum(i, place_in_row) for i in range(WIDE - 1)]

    def sum_rows():
        remote(
            partial_sums.at[1 - row],
            partial_sums.at[1 - row],
            pair_send.at[0],
            pair_recv.at[1 - row],
            other_row,
        ).wait_recv()
        pair_sums[place_in_row] = partial_sums[0] + partial_sums[1]
        for copy in psums:
            copy.start()

    plane_adapters = [adapters_ref[base + lax.rem(plane + step, PLANE)] for step in range(PLANE)]
    live_ref[...] = (
        lax.broadcasted_iota(jnp.int32, (1, 128), 1) < counts_ref[dp]
    ).astype(jnp.int32)

    hops = {
        (way, r): remote(
            hop_out.at[way, r - 1],
            hop_in.at[way, r - 1],
            hop_send.at[way, r - 1],
            hop_recv.at[way, r - 1],
            along((1 if way == 0 else -1) * (1 if r % 2 else 2)),
        )
        for group in groups[1:-1]
        for way, r in group
    }

    def plane_sum(way, r):
        n = chunk_of(way, r)
        y_copies[n].wait_recv()
        return [value + y_in[n, :, b].astype(F32) for b, value in enumerate(line_sum(way, r, half))]

    def arrived_sum(way, r, values):
        for child in (r + 1, r + 2):
            if (way, child) in hops:
                hops[way, child].wait_recv()
                values = [
                    value + hop_in[way, child - 1, :, b].astype(F32)
                    for b, value in enumerate(values)
                ]
        return values

    def send_round(group):
        for way, r in groups[group]:
            values = plane_sum(way, r)
            if r % 2 == 0:
                values = arrived_sum(way, r, values)
            for b, value in enumerate(values):
                hop_out[way, r - 1, :, b] = value.astype(WIRE)
            hops[way, r].start()

    def spread(batch, i, source, mate):
        first, count = slots_of_batch(batch)
        return remote(
            spread_out.at[i, pl.ds(first, count)],
            spread_in.at[source, pl.ds(first, count)],
            spread_send.at[batch, i],
            spread_recv.at[batch, source],
            mate,
        )

    def choose(block, adapter):
        result = block[0]
        for a in range(1, 4):
            result = jnp.where(adapter == a, block[a], result)
        return result

    spreads = []

    def place(block, slot):
        spread_in[plane, slot] = choose(block, plane_adapters[0])
        for i in range(PLANE - 1):
            spread_out[i, slot] = choose(block, plane_adapters[i + 1])

    def gather_pass(batch):
        for way in range(2):
            if (way, 2 * batch + 2) in blocks:
                blocks[way, 2 * batch + 2].wait_recv()
        if batch + 1 < ROUNDS:
            pass_round(batch + 1)

    def gather_spread(batch):
        if batch == 0:
            place(mine[...], 0)
        for r in (2 * batch + 1, 2 * batch + 2):
            for way in range(2):
                if (way, r) in blocks:
                    if r % 2:
                        blocks[way, r].wait_recv()
                    place(gathered[way, r - 1], 2 * r - 1 + way)
        for i in range(PLANE - 1):
            copy = spread(batch, i, plane, mate_ids[i])
            copy.start()
            spreads.append(copy)

    gather_pass(0)
    serve_across(6)
    serve_across(3)
    serve_across(2)
    serve_across(1)
    serve_across(0)
    gather_pass(1)
    send_round(1)
    gather_spread(0)
    gather_pass(2)
    gather_spread(1)
    sum_rows()
    send_round(2)
    gather_pass(3)
    gather_spread(2)
    gather_spread(3)
    send_round(3)

    for i, peer in enumerate(peers):
        psum(i, peer).wait_recv()
    shrunk = pair_sums[0]
    for i in range(1, WIDE):
        shrunk = shrunk + pair_sums[i]
    shrunk_ref[...] = shrunk.astype(BF16)

    for batch in range(ROUNDS):
        for i, mate in enumerate(mates):
            spread(batch, i, mate, mate_ids[i]).wait_recv()

    get_inverse.wait()

    @pl.loop(0, Z * PLANE, unroll=8)
    def _(k):
        owner = inverse[0, k]
        delta = lax.rem(owner // PLANE - z + Z, Z)
        slot = jnp.where(delta < STEPS, 2 * delta, 2 * Z - 1 - 2 * delta)
        natural[k] = spread_in[owner % PLANE, slot]

    @pl.loop(0, 1920 // LANES, unroll=5)
    def _(t):
        first = jnp.minimum((LANES * t) // FB, Z * PLANE - 6)
        offset = LANES * t - FB * first
        row = lax.broadcasted_iota(jnp.int32, (6 * PAD, LANES), 0)
        column = lax.broadcasted_iota(jnp.int32, (6 * PAD, LANES), 1)
        hit = (row - 2 * (row // PAD) == offset + column) & (row % PAD < FB)
        pick = jnp.where(hit, F32(1.0), F32(0.0)).astype(BF16)
        block = lax.dot_general(
            natural[pl.ds(first, 6)].reshape(6 * PAD, LANES),
            pick,
            (((0,), (0,)), ((), ())),
            preferred_element_type=F32,
        )
        factor[:, pl.ds(pl.multiple_of(t * LANES, LANES), LANES)] = block.astype(BF16)
    put_factor = local(factor, bt_ref, 10)

    values = plane_sum(0, 0)
    for way in range(2):
        values = arrived_sum(way, 0, values)
    for b, value in enumerate(values):
        final_out[b] = value
    final = remote(
        final_out.at[1 - core], final_in, final_send.at[0], final_recv.at[0], sibling
    )
    final.start()

    total_ref[pl.ds(2 * core, 2)] = final_out[core]
    final.wait_recv()
    total_ref[pl.ds(2 * (1 - core), 2)] = final_in[...]

    put_factor.wait()
    for copy in core_copies + used_y + psums + spreads + [pair, final]:
        copy.wait_send()
    for copy in list(early.values()) + list(hops.values()) + list(blocks.values()):
        copy.wait_send()


def exchange(adapters, table, counts, tokens, down, prior, grads):
    vmem = pl.BlockSpec(memory_space=pltpu.VMEM)
    hbm = pl.BlockSpec(memory_space=pltpu.HBM)
    dma = pltpu.SemaphoreType.DMA
    chunk = (PLANE, PAD, LANES)
    return pl.pallas_call(
        exchange_kernel,
        out_shape=(
            jax.ShapeDtypeStruct((LANES, 1920), BF16),
            jax.ShapeDtypeStruct((64, 128), BF16),
            jax.ShapeDtypeStruct((1, 128), jnp.int32),
            jax.ShapeDtypeStruct((4, PAD, LANES), F32),
        ),
        in_specs=[hbm] * 7,
        out_specs=(hbm, vmem, vmem, vmem),
        scratch_shapes=[
            pltpu.SMEM((64,), jnp.int32),
            pltpu.SMEM((64,), jnp.int32),
            pltpu.SMEM((64,), jnp.int32),
            pltpu.VMEM((64,), jnp.int32),
            pltpu.VMEM((128, 1024), BF16),
            pltpu.VMEM((4, 64, 1024), BF16),
            pltpu.VMEM((240, 64), F32),
            pltpu.VMEM((4, PAD, LANES), F32),
            pltpu.VMEM((4, PAD, LANES), BF16),
            pltpu.VMEM((PLANE * PAD, 2 * LANES), jnp.int32),
            pltpu.VMEM((1, 64), jnp.int32),
            pltpu.SMEM((1, 64), jnp.int32),
            pltpu.VMEM((2, LANES, 1920), BF16),
            pltpu.VMEM((2, LANES, 1920), BF16),
            pltpu.VMEM((Z * PLANE, 2, PAD, LANES), BF16),
            pltpu.VMEM((Z * PLANE, 2, PAD, LANES), BF16),
            pltpu.VMEM((2 * STEPS, 2) + chunk, BF16),
            pltpu.VMEM((2 * STEPS, 2) + chunk, BF16),
            pltpu.VMEM((Z, 2, 2, PAD, LANES), WIRE),
            pltpu.VMEM((Z, 2, 2, PAD, LANES), WIRE),
            pltpu.VMEM((2, 2) + (2,) + chunk, WIRE),
            pltpu.VMEM((2, 2) + (2,) + chunk, WIRE),
            pltpu.VMEM((2, DOWN, 2, 2, PAD, LANES), WIRE),
            pltpu.VMEM((2, DOWN, 2, 2, PAD, LANES), WIRE),
            pltpu.VMEM((2, DOWN, 4, PAD, LANES), BF16),
            pltpu.VMEM((PLANE - 1, Z, PAD, LANES), BF16),
            pltpu.VMEM((PLANE, Z, PAD, LANES), BF16),
            pltpu.VMEM((2, 2, PAD, LANES), F32),
            pltpu.VMEM((2, PAD, LANES), F32),
            pltpu.VMEM((2, 64, 128), F32),
            pltpu.VMEM((WIDE, 64, 128), F32),
            pltpu.VMEM((Z * PLANE, PAD, LANES), BF16),
            pltpu.VMEM((LANES, 1920), BF16),
            dma((11,)),
            dma((2 * STEPS,)),
            dma((2 * STEPS,)),
            dma((Z,)),
            dma((Z,)),
            dma((2, 2)),
            dma((2, 2)),
            dma((2, DOWN)),
            dma((2, DOWN)),
            dma((2, DOWN)),
            dma((2, DOWN)),
            dma((ROUNDS, PLANE - 1)),
            dma((ROUNDS, PLANE)),
            dma((1,)),
            dma((1,)),
            dma((1,)),
            dma((2,)),
            dma((WIDE - 1,)),
            dma((WIDE,)),
        ],
        compiler_params=pltpu.CompilerParams(
            collective_id=0,
            has_side_effects=True,
            vmem_limit_bytes=VMEM_LIMIT,
        ),
        cost_estimate=pl.CostEstimate(
            flops=2_000_000_000, bytes_accessed=8_000_000, transcendentals=0
        ),
        name="exchange",
    )(adapters, table, counts, tokens, down, prior, grads)


def adam_kernel(total_ref, prior_ref, first_ref, second_ref, b_ref, m_ref, v_ref):
    for a in range(4):
        for c in range(2):
            grad = total_ref[a, pl.ds(0, FB), pl.ds(64 * c, 64)]
            rows = pl.ds(2 * FB * a + c, FB, stride=2)
            new_m = BETA_ONE * first_ref[rows, :] + (1.0 - BETA_ONE) * grad
            new_v = BETA_TWO * second_ref[rows, :] + (1.0 - BETA_TWO) * grad * grad
            m_hat = new_m / (1.0 - BETA_ONE**ADAM_STEP)
            v_hat = new_v / (1.0 - BETA_TWO**ADAM_STEP)
            b_ref[rows, :] = prior_ref[rows, :] - LEARN_RATE * m_hat / (jnp.sqrt(v_hat) + EPSILON)
            m_ref[rows, :] = new_m
            v_ref[rows, :] = new_v


def adam(total, prior, first, second):
    vmem = pl.BlockSpec(memory_space=pltpu.VMEM)
    return pl.pallas_call(
        adam_kernel,
        out_shape=(jax.ShapeDtypeStruct((240, 64), F32),) * 3,
        in_specs=[vmem] * 4,
        out_specs=(vmem,) * 3,
        name="adam",
    )(total, prior, first, second)


def on_device(
    tokens,
    frozen_gate_up,
    frozen_down_factor,
    prior_b_factors,
    first_moment_owned,
    second_moment_owned,
    replica_gradients,
    adapter_of_block,
    live_row_count,
    owner_block_table,
):
    adapters, _, owned_rows, rank = prior_b_factors.shape
    width = replica_gradients.shape[3]

    def flat(array):
        return array.transpose(0, 2, 1, 3).reshape(adapters * owned_rows * 2, rank)

    def shaped(array):
        return array.reshape(adapters, owned_rows, 2, rank).transpose(0, 2, 1, 3)

    prior = flat(prior_b_factors)
    grads = (
        replica_gradients.reshape(adapters, 2, width, rank)
        .transpose(0, 1, 3, 2)
        .reshape(adapters, 2 * rank, width)
    )
    chosen, shrunk, live, total = exchange(
        adapter_of_block.reshape(-1),
        owner_block_table,
        live_row_count.reshape(-1),
        tokens,
        frozen_down_factor,
        prior,
        grads,
    )
    adapter_change = jnp.einsum(
        "rn,crg->ncg", shrunk, chosen.reshape(2, rank, width), preferred_element_type=F32
    )
    pre = frozen_gate_up.astype(F32) + ADAPTER_SCALE * adapter_change
    gated = jax.nn.silu(pre[:, 0]) * pre[:, 1]
    hidden = jnp.where((live[0] > 0)[:, None], gated, F32(0.0)).astype(BF16)
    new_b, new_m, new_v = adam(total, prior, flat(first_moment_owned), flat(second_moment_owned))
    return (shaped(new_b), shaped(new_m), shaped(new_v), hidden)


def solution(mesh):
    placed = (
        P("dp", "tensor"),
        P("dp", None, "tensor"),
        P(None, None, "tensor"),
        P(None, None, ("tensor", "dp"), None),
        P(None, None, ("tensor", "dp"), None),
        P(None, None, ("tensor", "dp"), None),
        P("dp", None, None, "tensor", None),
        P(),
        P(),
        P(),
    )
    return jax.shard_map(
        on_device,
        mesh=mesh,
        in_specs=placed,
        out_specs=(
            P(None, None, ("tensor", "dp"), None),
            P(None, None, ("tensor", "dp"), None),
            P(None, None, ("tensor", "dp"), None),
            P("dp", "tensor"),
        ),
        check_vma=False,
    )
```

```python
import functools

import jax
import jax.numpy as jnp
from jax import lax
from jax.experimental import pallas as pl
from jax.experimental.pallas import tpu as pltpu
from jax.sharding import PartitionSpec as P

ADAM_STEP = 20


ADAPTER_SCALE = 2.0
BETA_ONE = 0.9
BETA_TWO = 0.95
LEARN_RATE = 0.05
EPSILON = 1e-08

MESH = pl.DeviceIdType.MESH
Z = 16
PLANE = 4
WIDE = 4
DOWN = Z // 2
STEPS = Z // 2
ROUNDS = Z // 4
FB = 30
PAD = 32
LANES = 128
WIRE = jnp.bfloat16
VMEM_LIMIT = 60 * 1024 * 1024
F32 = jnp.float32
BF16 = jnp.bfloat16


def slots_of_batch(batch):
    return (0, 5) if batch == 0 else (4 * batch + 1, 4 if batch < ROUNDS - 1 else 3)


def exchange_kernel(
    adapters_hbm,
    table_hbm,
    counts_hbm,
    tokens_ref,
    down_ref,
    prior_ref,
    grads_ref,
    bt_ref,
    shrunk_ref,
    live_ref,
    total_ref,
    adapters_ref,
    table_ref,
    counts_ref,
    table_row_ref,
    tokens_in,
    down_in_all,
    prior_in,
    wide,
    mine,
    lag,
    inverse_row,
    inverse,
    own_half,
    other_half,
    own_terms,
    other_terms,
    core_out,
    core_in,
    y_out,
    y_in,
    early_out,
    early_in,
    hop_out,
    hop_in,
    gathered,
    spread_out,
    spread_in,
    final_out,
    final_in,
    partial_sums,
    pair_sums,
    natural,
    factor,
    local_sem,
    core_send,
    core_recv,
    y_send,
    y_recv,
    early_send,
    early_recv,
    hop_send,
    hop_recv,
    gather_send,
    gather_recv,
    spread_send,
    spread_recv,
    final_send,
    final_recv,
    pair_send,
    pair_recv,
    psum_send,
    psum_recv,
):
    dp = lax.axis_index("dp")
    tensor = lax.axis_index("tensor")
    z = dp // PLANE
    plane = dp % PLANE
    core = plane % 2
    half = plane // 2
    base = z * PLANE

    def along(distance):
        return (lax.rem(z + Z + distance, Z) * PLANE + plane, tensor)

    above, below = along(1), along(-1)
    sibling = (base + plane - core + (1 - core), tensor)
    across = (base + (1 - half) * 2 + core, tensor)
    mates = [lax.rem(plane + step, PLANE) for step in range(1, PLANE)]
    mate_ids = [(base + mate, tensor) for mate in mates]
    row, place_in_row = tensor // WIDE, tensor % WIDE
    other_row = (dp, (1 - row) * WIDE + place_in_row)
    peers = [lax.rem(place_in_row + step, WIDE) for step in range(1, WIDE)]
    peer_ids = [(dp, row * WIDE + peer) for peer in peers]

    barrier = pltpu.get_barrier_semaphore()
    everyone = [above, below, along(2), along(-2)] + mate_ids + peer_ids + [other_row]
    for device in everyone:
        pl.semaphore_signal(barrier, inc=1, device_id=device, device_id_type=MESH)

    def local(src, dst, i):
        copy = pltpu.make_async_copy(src, dst, local_sem.at[i])
        copy.start()
        return copy

    get_small = [
        local(adapters_hbm, adapters_ref, 6),
        local(table_hbm, table_ref, 7),
        local(counts_hbm, counts_ref, 8),
        local(table_hbm, table_row_ref, 9),
    ]
    get_prior = local(prior_ref, prior_in, 0)
    get_other = local(grads_ref.at[pl.ds(2 * (1 - core), 2)], other_half, 1)
    get_own = local(grads_ref.at[pl.ds(2 * core, 2)], own_half, 2)
    get_down = local(down_ref, down_in_all, 3)
    get_tokens = local(tokens_ref, tokens_in, 4)

    turn_row = lax.broadcasted_iota(jnp.int32, (PLANE * PAD, 2 * LANES), 0)
    turn_column = lax.broadcasted_iota(jnp.int32, (PLANE * PAD, 2 * LANES), 1)
    lag[...] = jnp.where(turn_row % PAD < FB, turn_column - turn_row + 2 * (turn_row // PAD), -1)

    def turn(half, terms):
        @pl.loop(0, Z, unroll=4)
        def _(q):
            window = pl.multiple_of(
                jnp.minimum((120 * q) // LANES * LANES, 1920 - 2 * LANES), LANES
            )
            offset = 120 * q - window
            pick = jnp.where(lag[...] == offset, F32(1.0), F32(0.0)).astype(BF16)
            block = lax.dot_general(
                pick,
                half[:, :, pl.ds(window, 2 * LANES)].reshape(2 * LANES, 2 * LANES),
                (((1,), (1,)), ((), ())),
                preferred_element_type=F32,
            ).astype(BF16)
            for p in range(2):
                terms[pl.ds(PLANE * q, PLANE), p] = block[:, p * LANES : (p + 1) * LANES].reshape(
                    PLANE, PAD, LANES
                )

    get_other.wait()
    turn(other_half, other_terms)

    wide[...] = jnp.zeros_like(wide)
    get_prior.wait()
    for a in range(4):
        for c in range(2):
            wide[a, pl.ds(0, FB), pl.ds(64 * c, 64)] = prior_in[
                pl.ds(2 * FB * a + c, FB, stride=2), :
            ]
    mine[...] = wide[...].astype(BF16)

    for copy in get_small:
        copy.wait()

    pl.semaphore_wait(barrier, len(everyone))

    def remote(src, dst, send, recv, device):
        return pltpu.make_async_remote_copy(
            src_ref=src,
            dst_ref=dst,
            send_sem=send,
            recv_sem=recv,
            device_id=device,
            device_id_type=MESH,
        )

    def pass_on(way, r):
        even = r - 1 if r % 2 else r - 2
        return remote(
            gathered.at[way, even - 1] if even else mine,
            gathered.at[way, r - 1],
            gather_send.at[way, r - 1],
            gather_recv.at[way, r - 1],
            along((1 if way == 0 else -1) * (r - even)),
        )

    blocks = {
        (way, r): pass_on(way, r)
        for r in range(1, Z // 2 + 1)
        for way in range(2)
        if (way, r) != (1, Z // 2)
    }

    def pass_round(batch):
        for r in (2 * batch + 2, 2 * batch + 1):
            for way in range(2):
                if (way, r) in blocks:
                    blocks[way, r].start()

    pass_round(0)

    def chunk_of(way, distance):
        return 2 * (Z // 2 - distance) + way if distance else 0

    def owners_of(way, distance):
        return PLANE * lax.rem(z + Z + (distance if way == 0 else -distance), Z)

    groups = [
        [(way, r) for r in (Z // 2 - 2 * k, Z // 2 - 1 - 2 * k) for way in range(2) if (way, r) != (0, Z // 2)]
        for k in range(Z // 4)
    ] + [[(0, 0)]]
    core_copies = [
        remote(core_out.at[n], core_in.at[n], core_send.at[n], core_recv.at[n], sibling)
        for n in range(Z)
    ]
    y_copies = [
        remote(y_out.at[n], y_in.at[n], y_send.at[n], y_recv.at[n], across) for n in range(Z)
    ]
    used_y = [y_copies[chunk_of(way, r)] for group in groups[1:] for way, r in group]

    def serve(group):
        for way, r in groups[group]:
            n, first = chunk_of(way, r), owners_of(way, r)
            for b in range(PLANE):
                core_out[n, :, b] = other_terms[table_ref[first + b]]
            core_copies[n].start()

    def chip_sum(way, r, side):
        n, first = chunk_of(way, r), owners_of(way, r) + 2 * side
        return [
            own_terms[table_ref[first + b]].astype(F32) + core_in[n, :, 2 * side + b].astype(F32)
            for b in range(2)
        ]

    early = {
        (way, r): remote(
            early_out.at[way, r - 7],
            early_in.at[way, r - 7],
            early_send.at[way, r - 7],
            early_recv.at[way, r - 7],
            along((1 if way == 0 else -1) * (r - 6)),
        )
        for way, r in groups[0]
    }

    def send_early():
        for way, r in groups[0]:
            core_copies[chunk_of(way, r)].wait_recv()
            for side in range(2):
                for b, value in enumerate(chip_sum(way, r, side)):
                    early_out[way, r - 7, :, 2 * side + b] = value.astype(WIRE)
            early[way, r].start()

    def line_sum(way, r, side):
        values = chip_sum(way, r, side)
        for child in (7, 8) if r == 6 else ():
            if (way, child) in early:
                values = [
                    value + early_in[way, child - 7, :, 2 * side + b].astype(F32)
                    for b, value in enumerate(values)
                ]
        return values

    def serve_across(r):
        for way in range(2 if r else 1):
            n = chunk_of(way, r)
            core_copies[n].wait_recv()
            for child in (7, 8) if r == 6 else ():
                if (way, child) in early:
                    early[way, child].wait_recv()
            for b, value in enumerate(line_sum(way, r, 1 - half)):
                y_out[n, :, b] = value.astype(WIRE)
            y_copies[n].start()

    serve(0)
    serve(1)

    get_own.wait()
    turn(own_half, own_terms)
    send_early()
    serve(2)
    serve_across(5)
    serve_across(4)
    serve(3)
    serve(4)

    owner_at = lax.broadcasted_iota(jnp.int32, (64, 64), 0)
    block_at = lax.broadcasted_iota(jnp.int32, (64, 64), 1)
    table_rows = jnp.broadcast_to(table_row_ref[...].reshape(1, 64), (64, 64))
    table_column = jnp.sum(jnp.where(owner_at == block_at, table_rows, 0), axis=1, keepdims=True)
    found = jnp.where(table_column == block_at, owner_at, 0)
    inverse_row[...] = jnp.sum(found, axis=0, keepdims=True)
    get_inverse = local(inverse_row, inverse, 5)

    get_down.wait()
    get_tokens.wait()
    partial_sums[row] = lax.dot_general(
        down_in_all[adapters_ref[dp]],
        tokens_in[...],
        (((1,), (1,)), ((), ())),
        preferred_element_type=F32,
    )
    pair = remote(
        partial_sums.at[row], partial_sums.at[row], pair_send.at[0], pair_recv.at[row], other_row
    )
    pair.start()

    def psum(i, source):
        return remote(
            pair_sums.at[source],
            pair_sums.at[source],
            psum_send.at[i],
            psum_recv.at[source],
            peer_ids[i],
        )

    psums = [psum(i, place_in_row) for i in range(WIDE - 1)]

    def sum_rows():
        remote(
            partial_sums.at[1 - row],
            partial_sums.at[1 - row],
            pair_send.at[0],
            pair_recv.at[1 - row],
            other_row,
        ).wait_recv()
        pair_sums[place_in_row] = partial_sums[0] + partial_sums[1]
        for copy in psums:
            copy.start()

    plane_adapters = [adapters_ref[base + lax.rem(plane + step, PLANE)] for step in range(PLANE)]
    live_ref[...] = (
        lax.broadcasted_iota(jnp.int32, (1, 128), 1) < counts_ref[dp]
    ).astype(jnp.int32)

    hops = {
        (way, r): remote(
            hop_out.at[way, r - 1],
            hop_in.at[way, r - 1],
            hop_send.at[way, r - 1],
            hop_recv.at[way, r - 1],
            along((1 if way == 0 else -1) * (1 if r % 2 else 2)),
        )
        for group in groups[1:-1]
        for way, r in group
    }

    def plane_sum(way, r):
        n = chunk_of(way, r)
        y_copies[n].wait_recv()
        return [value + y_in[n, :, b].astype(F32) for b, value in enumerate(line_sum(way, r, half))]

    def arrived_sum(way, r, values):
        for child in (r + 1, r + 2):
            if (way, child) in hops:
                hops[way, child].wait_recv()
                values = [
                    value + hop_in[way, child - 1, :, b].astype(F32)
                    for b, value in enumerate(values)
                ]
        return values

    def send_round(group):
        for way, r in groups[group]:
            values = plane_sum(way, r)
            if r % 2 == 0:
                values = arrived_sum(way, r, values)
            for b, value in enumerate(values):
                hop_out[way, r - 1, :, b] = value.astype(WIRE)
            hops[way, r].start()

    def spread(batch, i, source, mate):
        first, count = slots_of_batch(batch)
        return remote(
            spread_out.at[i, pl.ds(first, count)],
            spread_in.at[source, pl.ds(first, count)],
            spread_send.at[batch, i],
            spread_recv.at[batch, source],
            mate,
        )

    def choose(block, adapter):
        result = block[0]
        for a in range(1, 4):
            result = jnp.where(adapter == a, block[a], result)
        return result

    spreads = []

    def place(block, slot):
        spread_in[plane, slot] = choose(block, plane_adapters[0])
        for i in range(PLANE - 1):
            spread_out[i, slot] = choose(block, plane_adapters[i + 1])

    def gather_pass(batch):
        for way in range(2):
            if (way, 2 * batch + 2) in blocks:
                blocks[way, 2 * batch + 2].wait_recv()
        if batch + 1 < ROUNDS:
            pass_round(batch + 1)

    def gather_spread(batch):
        if batch == 0:
            place(mine[...], 0)
        for r in (2 * batch + 1, 2 * batch + 2):
            for way in range(2):
                if (way, r) in blocks:
                    if r % 2:
                        blocks[way, r].wait_recv()
                    place(gathered[way, r - 1], 2 * r - 1 + way)
        for i in range(PLANE - 1):
            copy = spread(batch, i, plane, mate_ids[i])
            copy.start()
            spreads.append(copy)

    gather_pass(0)
    serve_across(6)
    serve_across(3)
    serve_across(2)
    serve_across(1)
    serve_across(0)
    gather_pass(1)
    send_round(1)
    gather_spread(0)
    gather_pass(2)
    gather_spread(1)
    sum_rows()
    send_round(2)
    gather_pass(3)
    gather_spread(2)
    gather_spread(3)
    send_round(3)

    for i, peer in enumerate(peers):
        psum(i, peer).wait_recv()
    shrunk = pair_sums[0]
    for i in range(1, WIDE):
        shrunk = shrunk + pair_sums[i]
    shrunk_ref[...] = shrunk.astype(BF16)

    for batch in range(ROUNDS):
        for i, mate in enumerate(mates):
            spread(batch, i, mate, mate_ids[i]).wait_recv()

    get_inverse.wait()

    @pl.loop(0, Z * PLANE, unroll=8)
    def _(k):
        owner = inverse[0, k]
        delta = lax.rem(owner // PLANE - z + Z, Z)
        slot = jnp.where(delta < STEPS, 2 * delta, 2 * Z - 1 - 2 * delta)
        natural[k] = spread_in[owner % PLANE, slot]

    @pl.loop(0, 1920 // LANES, unroll=5)
    def _(t):
        first = jnp.minimum((LANES * t) // FB, Z * PLANE - 6)
        offset = LANES * t - FB * first
        row = lax.broadcasted_iota(jnp.int32, (6 * PAD, LANES), 0)
        column = lax.broadcasted_iota(jnp.int32, (6 * PAD, LANES), 1)
        hit = (row - 2 * (row // PAD) == offset + column) & (row % PAD < FB)
        pick = jnp.where(hit, F32(1.0), F32(0.0)).astype(BF16)
        block = lax.dot_general(
            natural[pl.ds(first, 6)].reshape(6 * PAD, LANES),
            pick,
            (((0,), (0,)), ((), ())),
            preferred_element_type=F32,
        )
        factor[:, pl.ds(pl.multiple_of(t * LANES, LANES), LANES)] = block.astype(BF16)
    put_factor = local(factor, bt_ref, 10)

    values = plane_sum(0, 0)
    for way in range(2):
        values = arrived_sum(way, 0, values)
    for b, value in enumerate(values):
        final_out[b] = value
    final = remote(
        final_out.at[1 - core], final_in, final_send.at[0], final_recv.at[0], sibling
    )
    final.start()

    total_ref[pl.ds(2 * core, 2)] = final_out[core]
    final.wait_recv()
    total_ref[pl.ds(2 * (1 - core), 2)] = final_in[...]

    put_factor.wait()
    for copy in core_copies + used_y + psums + spreads + [pair, final]:
        copy.wait_send()
    for copy in list(early.values()) + list(hops.values()) + list(blocks.values()):
        copy.wait_send()


def exchange(adapters, table, counts, tokens, down, prior, grads):
    vmem = pl.BlockSpec(memory_space=pltpu.VMEM)
    hbm = pl.BlockSpec(memory_space=pltpu.HBM)
    dma = pltpu.SemaphoreType.DMA
    chunk = (PLANE, PAD, LANES)
    return pl.pallas_call(
        exchange_kernel,
        out_shape=(
            jax.ShapeDtypeStruct((LANES, 1920), BF16),
            jax.ShapeDtypeStruct((64, 128), BF16),
            jax.ShapeDtypeStruct((1, 128), jnp.int32),
            jax.ShapeDtypeStruct((4, PAD, LANES), F32),
        ),
        in_specs=[hbm] * 7,
        out_specs=(hbm, vmem, vmem, vmem),
        scratch_shapes=[
            pltpu.SMEM((64,), jnp.int32),
            pltpu.SMEM((64,), jnp.int32),
            pltpu.SMEM((64,), jnp.int32),
            pltpu.VMEM((64,), jnp.int32),
            pltpu.VMEM((128, 1024), BF16),
            pltpu.VMEM((4, 64, 1024), BF16),
            pltpu.VMEM((240, 64), F32),
            pltpu.VMEM((4, PAD, LANES), F32),
            pltpu.VMEM((4, PAD, LANES), BF16),
            pltpu.VMEM((PLANE * PAD, 2 * LANES), jnp.int32),
            pltpu.VMEM((1, 64), jnp.int32),
            pltpu.SMEM((1, 64), jnp.int32),
            pltpu.VMEM((2, LANES, 1920), BF16),
            pltpu.VMEM((2, LANES, 1920), BF16),
            pltpu.VMEM((Z * PLANE, 2, PAD, LANES), BF16),
            pltpu.VMEM((Z * PLANE, 2, PAD, LANES), BF16),
            pltpu.VMEM((2 * STEPS, 2) + chunk, BF16),
            pltpu.VMEM((2 * STEPS, 2) + chunk, BF16),
            pltpu.VMEM((Z, 2, 2, PAD, LANES), WIRE),
            pltpu.VMEM((Z, 2, 2, PAD, LANES), WIRE),
            pltpu.VMEM((2, 2) + (2,) + chunk, WIRE),
            pltpu.VMEM((2, 2) + (2,) + chunk, WIRE),
            pltpu.VMEM((2, DOWN, 2, 2, PAD, LANES), WIRE),
            pltpu.VMEM((2, DOWN, 2, 2, PAD, LANES), WIRE),
            pltpu.VMEM((2, DOWN, 4, PAD, LANES), BF16),
            pltpu.VMEM((PLANE - 1, Z, PAD, LANES), BF16),
            pltpu.VMEM((PLANE, Z, PAD, LANES), BF16),
            pltpu.VMEM((2, 2, PAD, LANES), F32),
            pltpu.VMEM((2, PAD, LANES), F32),
            pltpu.VMEM((2, 64, 128), F32),
            pltpu.VMEM((WIDE, 64, 128), F32),
            pltpu.VMEM((Z * PLANE, PAD, LANES), BF16),
            pltpu.VMEM((LANES, 1920), BF16),
            dma((11,)),
            dma((2 * STEPS,)),
            dma((2 * STEPS,)),
            dma((Z,)),
            dma((Z,)),
            dma((2, 2)),
            dma((2, 2)),
            dma((2, DOWN)),
            dma((2, DOWN)),
            dma((2, DOWN)),
            dma((2, DOWN)),
            dma((ROUNDS, PLANE - 1)),
            dma((ROUNDS, PLANE)),
            dma((1,)),
            dma((1,)),
            dma((1,)),
            dma((2,)),
            dma((WIDE - 1,)),
            dma((WIDE,)),
        ],
        compiler_params=pltpu.CompilerParams(
            collective_id=0,
            has_side_effects=True,
            vmem_limit_bytes=VMEM_LIMIT,
        ),
        cost_estimate=pl.CostEstimate(
            flops=2_000_000_000, bytes_accessed=8_000_000, transcendentals=0
        ),
        name="exchange",
    )(adapters, table, counts, tokens, down, prior, grads)


def adam_kernel(total_ref, prior_ref, first_ref, second_ref, b_ref, m_ref, v_ref):
    for a in range(4):
        for c in range(2):
            grad = total_ref[a, pl.ds(0, FB), pl.ds(64 * c, 64)]
            rows = pl.ds(2 * FB * a + c, FB, stride=2)
            new_m = BETA_ONE * first_ref[rows, :] + (1.0 - BETA_ONE) * grad
            new_v = BETA_TWO * second_ref[rows, :] + (1.0 - BETA_TWO) * grad * grad
            m_hat = new_m / (1.0 - BETA_ONE**ADAM_STEP)
            v_hat = new_v / (1.0 - BETA_TWO**ADAM_STEP)
            b_ref[rows, :] = prior_ref[rows, :] - LEARN_RATE * m_hat / (jnp.sqrt(v_hat) + EPSILON)
            m_ref[rows, :] = new_m
            v_ref[rows, :] = new_v


def adam(total, prior, first, second):
    vmem = pl.BlockSpec(memory_space=pltpu.VMEM)
    return pl.pallas_call(
        adam_kernel,
        out_shape=(jax.ShapeDtypeStruct((240, 64), F32),) * 3,
        in_specs=[vmem] * 4,
        out_specs=(vmem,) * 3,
        name="adam",
    )(total, prior, first, second)


def on_device(
    tokens,
    frozen_gate_up,
    frozen_down_factor,
    prior_b_factors,
    first_moment_owned,
    second_moment_owned,
    replica_gradients,
    adapter_of_block,
    live_row_count,
    owner_block_table,
):
    adapters, _, owned_rows, rank = prior_b_factors.shape
    width = replica_gradients.shape[3]

    def flat(array):
        return array.transpose(0, 2, 1, 3).reshape(adapters * owned_rows * 2, rank)

    def shaped(array):
        return array.reshape(adapters, owned_rows, 2, rank).transpose(0, 2, 1, 3)

    prior = flat(prior_b_factors)
    grads = (
        replica_gradients.reshape(adapters, 2, width, rank)
        .transpose(0, 1, 3, 2)
        .reshape(adapters, 2 * rank, width)
    )
    chosen, shrunk, live, total = exchange(
        adapter_of_block.reshape(-1),
        owner_block_table,
        live_row_count.reshape(-1),
        tokens,
        frozen_down_factor,
        prior,
        grads,
    )
    adapter_change = jnp.einsum(
        "rn,crg->ncg", shrunk, chosen.reshape(2, rank, width), preferred_element_type=F32
    )
    pre = frozen_gate_up.astype(F32) + ADAPTER_SCALE * adapter_change
    gated = jax.nn.silu(pre[:, 0]) * pre[:, 1]
    hidden = jnp.where((live[0] > 0)[:, None], gated, F32(0.0)).astype(BF16)
    new_b, new_m, new_v = adam(total, prior, flat(first_moment_owned), flat(second_moment_owned))
    return (shaped(new_b), shaped(new_m), shaped(new_v), hidden)


def solution(mesh):
    placed = (
        P("dp", "tensor"),
        P("dp", None, "tensor"),
        P(None, None, "tensor"),
        P(None, None, ("tensor", "dp"), None),
        P(None, None, ("tensor", "dp"), None),
        P(None, None, ("tensor", "dp"), None),
        P("dp", None, None, "tensor", None),
        P(),
        P(),
        P(),
    )
    return jax.shard_map(
        on_device,
        mesh=mesh,
        in_specs=placed,
        out_specs=(
            P(None, None, ("tensor", "dp"), None),
            P(None, None, ("tensor", "dp"), None),
            P(None, None, ("tensor", "dp"), None),
            P("dp", "tensor"),
        ),
        check_vma=False,
    )
```
